512 devices in a mesh: gx: 16 (over x, y), gy: 16 (over z_lo, core), var: 2 (over z_hi).
Axes of the slice: x: 4, y: 4, z: 16 (z_hi: 2, z_lo: 8; z = z_hi * 8 + z_lo), core: 2. Of those that a mesh axis runs over, the one named last changes fastest.
Arguments:
- field: bfloat16 [4, 1024, 1024, 128], P('var', 'gx', 'gy'), may hold values from -6 to 6
- probe_first: bfloat16 [1024, 40], P('gx'), may hold values from -0.1875 to 0.1875
- probe_second: bfloat16 [1024, 40], P('gy'), may hold values from -0.1875 to 0.1875
- probe_depth: bfloat16 [128, 40], replicated, may hold values from -0.5 to 0.5
- probe_vars: bfloat16 [4, 40], P('var'), may hold values from -3 to 3
- shrink_first: bfloat16 [48, 1024], P(None, 'gx'), may hold values from -0.25 to 0.25
- shrink_second: bfloat16 [48, 1024], P(None, 'gy'), may hold values from -0.25 to 0.25
- shrink_depth: bfloat16 [48, 128], replicated, may hold values from -0.5 to 0.5
- shrink_vars: bfloat16 [4, 4], P(None, 'var'), may hold values from -4 to 4
Outputs:
- range_first: float32 [1024, 40], P('gx')
- range_second: float32 [1024, 40], P('gy')
- range_depth: float32 [128, 40], replicated
- core_sketch: float32 [4, 48, 48, 48], P('var', 'gx', 'gy')
The draws below stay inside these ranges and needn't reach their ends.
All inputs are finite; a program needn't handle non-finite values.
Results may differ from the reference program's by a relative error of at most 0.0036.
Values sent between devices are 32-bit elements; how exact they have to be, the bound alone decides.
A program may use at most 64 MiB of HBM per device.

```python
import jax
import jax.numpy as jnp
from jax import lax

NZ = 128
V = 4
R = 40
K = 48
KV = 4
NX = 1024
NY = 1024


def with_spikes(result, stream_key, source, target, blocks, factor):
    def block_of(axis_at):
        return (jnp.arange(result.shape[axis_at]) // (result.shape[axis_at] // blocks)).reshape((-1,) + (1,) * (result.ndim - 1 - axis_at))

    first = jax.random.permutation(stream_key, blocks)[block_of(target)]
    other_side = (block_of(target) + blocks // 2) % blocks
    return jnp.where((block_of(source) == first) | (block_of(source) == other_side), factor * result, result)


def steps_of(rng, dims, pieces, least, largest):
    level, own = 1.0, jax.random.fold_in(rng, 6)
    for dim, parts in pieces:
        draws = jnp.exp(jax.random.uniform(jax.random.fold_in(own, dim), (parts,), jnp.float32, least / len(pieces), largest / len(pieces)))
        level = level * jnp.repeat(draws, dims[dim] // parts).reshape([-1 if axis == dim else 1 for axis in range(len(dims))])
    return level


def centred(rng, shape, width, reach, split=(), dtype=jnp.bfloat16):
    loudness = steps_of(rng, shape, split, -0.22, 0.18) if split else 1.0
    drawn = jax.random.normal(rng, shape, jnp.float32) * width * loudness
    return jnp.minimum(jnp.maximum(drawn, -reach), reach).astype(dtype)


def heavy_noise(stream_key, dims, deviation, bound, shards, heavy, dtype=jnp.bfloat16):
    drawn = deviation * jax.random.normal(stream_key, dims, jnp.float32)
    if shards:
        drawn = drawn * steps_of(stream_key, dims, shards, -0.22, 0.18)
    return jnp.clip(with_spikes(drawn, jax.random.fold_in(stream_key, 3), *heavy), -bound, bound).astype(dtype)


def setup_inputs(seed: int = 0) -> dict:
    seeds = jax.random.split(jax.random.key(seed), 10)
    field = heavy_noise(seeds[0], (V, NX, NY, NZ), 1.0, 6.0, ((0, 2), (1, 16), (2, 16)), (2, 1, 16, 2.0))
    probe_first = centred(seeds[1], (NX, R), NX ** -0.5, 0.1875, ((0, 16),))
    probe_second = centred(seeds[2], (NY, R), NY ** -0.5, 0.1875, ((0, 16),))
    probe_depth = centred(seeds[3], (NZ, R), NZ ** -0.5, 0.5)
    probe_vars = centred(seeds[4], (V, R), V ** -0.5, 3.0, ((0, 2),))
    shrink_first = heavy_noise(seeds[5], (K, NX), NX ** -0.5, 0.25, ((1, 16),), (1, 0, 16, 2.0))
    shrink_second = heavy_noise(seeds[6], (K, NY), NY ** -0.5, 0.25, ((1, 16),), (1, 0, 16, 2.0))
    shrink_depth = centred(seeds[7], (K, NZ), NZ ** -0.5, 0.5)
    shrink_vars = heavy_noise(seeds[8], (KV, V), V ** -0.5, 4.0, ((1, 2),), (1, 0, 2, 2.0))
    return dict(field=field, probe_first=probe_first, probe_second=probe_second, probe_depth=probe_depth, probe_vars=probe_vars, shrink_first=shrink_first, shrink_second=shrink_second, shrink_depth=shrink_depth, shrink_vars=shrink_vars)


HIGH = lax.Precision.HIGHEST


def reference(field, probe_first, probe_second, probe_depth, probe_vars, shrink_first, shrink_second, shrink_depth, shrink_vars):
    first32 = probe_first.astype(jnp.float32)
    second32 = probe_second.astype(jnp.float32)
    shrink_one = shrink_first.astype(jnp.float32)
    shrink_two = shrink_second.astype(jnp.float32)

    def per_variable(inputs):
        plane, var_row = inputs
        flat = plane.reshape(NX * NY, NZ)
        probed = jnp.dot(flat, probe_depth, preferred_element_type=jnp.float32).reshape(NX, NY, R)
        compressed = jnp.dot(flat, shrink_depth.T, preferred_element_type=jnp.float32).astype(jnp.bfloat16).reshape(NX, NY, K)
        var_scale = var_row.astype(jnp.float32)
        part_first = jnp.einsum('ijr,jr->ir', probed, second32 * var_scale, precision=HIGH)
        part_second = jnp.einsum('ijr,ir->jr', probed, first32 * var_scale, precision=HIGH)
        tested = (first32[:, None, :] * second32[None, :, :] * var_scale).astype(jnp.bfloat16).reshape(NX * NY, R)
        part_depth = jnp.dot(flat.T, tested, preferred_element_type=jnp.float32)
        mixed = jnp.einsum('ai,ijc->ajc', shrink_one, compressed.astype(jnp.float32), precision=HIGH)
        core_part = jnp.einsum('bj,ajc->abc', shrink_two, mixed, precision=HIGH)
        return part_first, part_second, part_depth, core_part

    parts_first, parts_second, parts_depth, core_parts = lax.map(per_variable, (field, probe_vars))
    core_sketch = jnp.einsum('wv,vabc->wabc', shrink_vars.astype(jnp.float32), core_parts, precision=HIGH)
    return jnp.sum(parts_first, axis=0), jnp.sum(parts_second, axis=0), jnp.sum(parts_depth, axis=0), core_sketch
```

```python
import jax
import jax.numpy as jnp
from jax import lax
from jax.experimental import pallas as pl
from jax.experimental.pallas import tpu as pltpu
from jax.sharding import PartitionSpec as P

F32 = jnp.float32
BF16 = jnp.bfloat16
MESH = pl.DeviceIdType.MESH

NX, NY, NZ = 4, 4, 16
GX = NX * NY
HALF = NZ // 2
PLANE = [
    (2, 2), (2, 1), (1, 2), (2, 3), (3, 2), (1, 1), (3, 3), (1, 3), (3, 1),
    (2, 0), (0, 2), (1, 0), (0, 1), (3, 0), (0, 3),
]
LINE = [8, 7, 9, 6, 10, 5, 11, 4, 12, 3, 13, 2, 14, 1, 15]
CHUNKS = 2
ZC = HALF // CHUNKS


def dot(a, b):
    return jnp.dot(a, b, preferred_element_type=F32)


def iota(shape, axis):
    return lax.broadcasted_iota(jnp.int32, shape, axis)


def kernel(
    field,
    probe_first,
    probe_second,
    probe_depth,
    probe_vars,
    shrink_first,
    shrink_second,
    shrink_depth,
    shrink_vars,
    out_first,
    out_second,
    out_depth,
    out_core,
    held,
    pad,
    joined,
    spread,
    mix,
    stage,
    mixed,
    weight_first,
    weight_second,
    tall_first,
    tall_second,
    tall_vars,
    rows_first,
    rows_second,
    core_away,
    core_own,
    core_sib,
    core_sum,
    core_plane,
    core_tiles,
    core_line,
    depth_parts,
    depth_sib,
    depth_sum,
    depth_plane,
    depth_tile,
    depth_line,
    depth_row,
    depth_back,
    first_pack,
    first_sib,
    first_sum,
    first_line,
    first_whole,
    second_pack,
    second_var,
    second_sum,
    second_plane,
    load_sem,
    pair_send,
    pair_recv,
    core_send,
    core_recv,
    plane_send,
    plane_recv,
    line_send,
    line_recv,
    dplane_send,
    dplane_recv,
    dline_send,
    dline_recv,
    drow_send,
    drow_recv,
    fline_send,
    fline_recv,
    splane_send,
    splane_recv,
):
    gx, gy, half = lax.axis_index("gx"), lax.axis_index("gy"), lax.axis_index("var")
    x, y = gx // NY, gx % NY
    z, core = half * HALF + gy // 2, gy % 2

    def in_plane(dx, dy):
        return ((x + dx) % NX) * NY + (y + dy) % NY

    def at_plane(there):
        return (there, gy, half)

    def at_line(there):
        return (gx, (there % HALF) * 2 + core, there // HALF)

    sibling = (gx, gy + 1 - 2 * core, half)
    partner = (gx, gy, 1 - half)

    barrier = pltpu.get_barrier_semaphore()
    for dz in LINE:
        pl.semaphore_signal(barrier, inc=1, device_id=at_line((z + dz) % NZ), device_id_type=MESH)
    for dx, dy in PLANE:
        pl.semaphore_signal(barrier, inc=1, device_id=at_plane(in_plane(dx, dy)), device_id_type=MESH)
    pl.semaphore_signal(barrier, inc=1, device_id=sibling, device_id_type=MESH)

    def load(g):
        rows = pl.ds(g * 8, 8)
        return pltpu.make_async_copy(field.at[:, rows], held.at[:, rows], load_sem.at[g])

    for g in range(8):
        load(g).start()

    def send(src, dst, send_sem, recv_sem, device):
        copy = pltpu.make_async_remote_copy(
            src_ref=src, dst_ref=dst, send_sem=send_sem, recv_sem=recv_sem, device_id=device, device_id_type=MESH
        )
        copy.start()
        return copy

    lane = iota((128, 128), 1)
    row = iota((128, 128), 0)
    zeros = jnp.zeros((128, 128), F32)

    pad[...] = zeros
    pad[0:48, :] = shrink_depth[...].astype(F32)
    pad[48:96, :] = shrink_depth[...].astype(F32)
    turned = pad[...].T
    joined[0:128, 0:128] = jnp.where(lane < 48, turned, 0.0).astype(BF16)
    joined[128:256, 0:128] = jnp.where(lane >= 48, turned, 0.0).astype(BF16)
    pad[...] = zeros
    pad[:, 0:40] = probe_depth[...].astype(F32)
    wide = pad[...]
    joined[0:128, 128:256] = wide.astype(BF16)
    joined[128:256, 128:256] = pltpu.roll(wide, 64, 1).astype(BF16)

    pad[...] = zeros
    pad[0:2, 0:40] = probe_vars[...].astype(F32)
    both = pad[0:8, :]
    vars_row = both[0:1, :] + pltpu.roll(both, 64, 1)[1:2, :]
    tall_vars[0] = jnp.broadcast_to(both[0:1, :], (128, 128)).T[0:40, :]
    tall_vars[1] = jnp.broadcast_to(both[1:2, :], (128, 128)).T[0:40, :]
    pad[...] = zeros
    pad[0:64, 0:40] = probe_first[...].astype(F32)
    wide = pad[0:64, :]
    weight_first[...] = (wide + pltpu.roll(wide, 64, 1)) * vars_row
    tall_first[...] = pad[...].T[0:40, 0:64].astype(BF16)
    pad[...] = zeros
    pad[0:64, 0:40] = probe_second[...].astype(F32)
    pad[64:128, 0:40] = probe_second[...].astype(F32)
    wide = pad[0:64, :]
    weight_second[...] = (wide + pltpu.roll(wide, 64, 1)) * vars_row
    tall_second[...] = pad[...].T[0:40, :]

    for q in range(4):
        pad[...] = zeros
        pad[0:48, 0:64] = shrink_second[...].astype(F32)
        block = pad[0:48, :]
        if q % 2:
            block = pltpu.roll(block, 64, 1)
        spread[q * 48 : q * 48 + 48, (q // 2) * 128 : (q // 2) * 128 + 128] = block.astype(BF16)
        spread[q * 48 : q * 48 + 48, (1 - q // 2) * 128 : (1 - q // 2) * 128 + 128] = jnp.zeros((48, 128), BF16)

    pad[...] = zeros
    pad[0:48, 0:64] = shrink_first[...].astype(F32)
    wide = pad[0:48, :]
    twice = (wide + pltpu.roll(wide, 64, 1)).astype(BF16)
    at = iota((128, 48), 0)
    col = iota((128, 48), 1)
    each = dot(jnp.where(col == 3 * (at // 8) + (at % 8) % 3, 1.0, 0.0).astype(BF16), twice)
    ninth = dot(jnp.where(col == 3 * (at // 8) + 2, 1.0, 0.0).astype(BF16), twice)
    place = row % 8
    left = lane < 64
    third = place // 3
    blocks = [
        jnp.where(third == jnp.where(left, 0, 1), each, 0.0),
        jnp.where(left, jnp.where(third == 2, each, 0.0), jnp.where(place == 0, ninth, 0.0)),
        jnp.where(place == jnp.where(left, 1, 2), ninth, 0.0),
    ]
    for q in range(3):
        mix[:, q * 128 : q * 128 + 128] = blocks[q].astype(BF16)
        mix[:, (q + 3) * 128 : (q + 3) * 128 + 128] = blocks[q].astype(BF16)

    second_pack[32:40, :] = jnp.zeros((8, 128), F32)
    second_pack[32:36, 0:2] = shrink_vars[...].astype(F32)

    def depth_step(g, total):
        load(g).wait()
        lanes = iota((64, 512), 1)
        pick = jnp.where(iota((64, 512), 0) == g * 8 + lanes // 64, 1.0, 0.0).astype(BF16)
        firsts = dot(tall_first[...], pick)
        seconds = tall_second[...]
        product = firsts * jnp.concatenate([seconds] * 4, axis=1)
        for v in range(2):
            scale = jnp.concatenate([tall_vars[v]] * 4, axis=1)
            tested = (product * scale).astype(BF16)
            total = total + dot(tested, held[v, pl.ds(g * 8, 8)].reshape(512, 128))
        return total

    depth_total = lax.fori_loop(0, 8, depth_step, jnp.zeros((40, 128), F32))
    depth_parts[...] = jnp.zeros((8, 8, 128), F32)
    for g in range(8):
        depth_parts[g, 0:5, :] = depth_total[5 * g : 5 * g + 5, :]

    def field_step(g, total):
        rows = pl.ds(g * 8, 8)
        flat = jnp.concatenate([held[0, rows].reshape(512, 128), held[1, rows].reshape(512, 128)], axis=1)
        product = dot(flat, joined[...])
        compressed = product[:, 0:128].astype(BF16)
        probed = product[:, 128:256].reshape(8, 64, 128)
        for q in range(2):
            stage[pl.ds(pl.multiple_of(g * 384 + q * 192, 64), 192), :] = dot(
                spread[...], compressed[q * 256 : q * 256 + 256, :]
            )
        firsts = weight_first[rows, :]
        seconds = weight_second[...]
        sums = []
        for i in range(8):
            total = total + probed[i] * firsts[i : i + 1, :]
            sums.append(jnp.sum(probed[i] * seconds, axis=0, keepdims=True))
        rows_first[rows, :] = jnp.concatenate(sums, axis=0)
        return total

    rows_second[...] = lax.fori_loop(0, 8, field_step, jnp.zeros((64, 128), F32))

    def pack(rows):
        rows = rows + pltpu.roll(rows, 64, 1)
        return jnp.where(iota((32, 128), 1) < 64, rows[0:32], rows[32:64])

    first_pack[...] = pack(rows_first[...]).reshape(2, 16, 128)
    second_pack[0:32, :] = pack(rows_second[...])

    def core_step(side, target):
        def body(s, _):
            for t in range(2):
                for b in range(3):
                    part = stage[pl.ds((s * 2 + t) * 6 + 3 * side + b, 64, stride=48), :]
                    parts = [(b, part)]
                    if b == 2:
                        for u in range(3):
                            moved = pltpu.roll(part, 96 - 32 * u, 1)
                            parts.append((3 + u, jnp.where(iota((64, 128), 1) >= 96, moved, 0.0)))
                    for at, value in parts:
                        high = value.astype(BF16)
                        low = (value - high.astype(F32)).astype(BF16)
                        mixed[at * 64 : at * 64 + 64, t * 128 : t * 128 + 128] = high
                        mixed[384 + at * 64 : 384 + at * 64 + 64, t * 128 : t * 128 + 128] = low
            result = dot(mix[...], mixed[...])
            for t in range(2):
                to = s * 2 + t
                target[to // ZC, :, to % ZC] = result[:, t * 128 : t * 128 + 128].reshape(GX, 8, 128)
            return 0

        lax.fori_loop(0, 4, body, 0)

    core_step(1 - core, core_away)

    pl.semaphore_wait(barrier, len(LINE) + len(PLANE) + 1)

    waits = []
    there = 1 - core
    pair_depth = send(
        depth_parts.at[pl.ds(there * 4, 4)], depth_sib, pair_send.at[0], pair_recv.at[0], sibling
    )
    pair_first = send(first_pack.at[there], first_sib, pair_send.at[1], pair_recv.at[1], sibling)
    pair_core = [
        send(core_away.at[q], core_sib.at[q], core_send.at[q], core_recv.at[q], sibling) for q in range(CHUNKS)
    ]
    pair_var = send(second_pack, second_var, pair_send.at[2], pair_recv.at[2], partner)
    core_step(core, core_own)

    pair_depth.wait_recv()
    depth_sum[...] = depth_parts[pl.ds(core * 4, 4)] + depth_sib[...]
    for i, (dx, dy) in enumerate(PLANE):
        to = in_plane(dx, dy)
        waits.append(
            send(depth_sum.at[to // NY], depth_plane.at[gx], dplane_send.at[i], dplane_recv.at[gx], at_plane(to))
        )
    depth_plane[gx] = depth_sum[x]

    pair_first.wait_recv()
    first_sum[...] = first_pack[core] + first_sib[...]
    for i, dz in enumerate(LINE):
        waits.append(
            send(first_sum, first_line.at[z], fline_send.at[i], fline_recv.at[z], at_line((z + dz) % NZ))
        )
    first_line[z] = first_sum[...]

    for q in range(CHUNKS):
        pair_core[q].wait_recv()
        core_sum[q] = core_own[q] + core_sib[q]
        for i, (dx, dy) in enumerate(PLANE):
            to = in_plane(dx, dy)
            waits.append(
                send(
                    core_sum.at[q, to],
                    core_plane.at[q, gx],
                    plane_send.at[q, i],
                    plane_recv.at[q, gx],
                    at_plane(to),
                )
            )
        core_plane[q, gx] = core_sum[q, gx]

    def received(dst, sem):
        pltpu.make_async_remote_copy(
            src_ref=dst, dst_ref=dst, send_sem=sem, recv_sem=sem, device_id=sibling, device_id_type=MESH
        ).wait_recv()

    for dx, dy in PLANE:
        of = in_plane(dx, dy)
        received(depth_plane.at[of], dplane_recv.at[of])
    depth_tile[...] = jnp.sum(depth_plane[...], axis=0)
    for i, dz in enumerate(LINE):
        waits.append(
            send(depth_tile, depth_line.at[z], dline_send.at[i], dline_recv.at[z], at_line((z + dz) % NZ))
        )
    depth_line[z] = depth_tile[...]

    pair_var.wait_recv()
    second_sum[...] = second_pack[0:32, :] + second_var[0:32, :]
    for i, (dx, dy) in enumerate(PLANE):
        waits.append(
            send(second_sum, second_plane.at[gx], splane_send.at[i], splane_recv.at[gx], at_plane(in_plane(dx, dy)))
        )
    second_plane[gx] = second_sum[...]

    for q in range(CHUNKS):
        for dx, dy in PLANE:
            of = in_plane(dx, dy)
            received(core_plane.at[q, of], plane_recv.at[q, of])
        core_tiles[q * ZC : q * ZC + ZC] = jnp.sum(core_plane[q], axis=0)
    for i, dz in enumerate(LINE):
        to = (z + dz) % NZ
        waits.append(send(core_tiles.at[to % HALF], core_line.at[z], line_send.at[i], line_recv.at[z], at_line(to)))
    core_line[z] = core_tiles[z % HALF]

    for dz in LINE:
        of = (z + dz) % NZ
        received(depth_line.at[of], dline_recv.at[of])
    depth_row[x] = jnp.sum(depth_line[...], axis=0)
    for i, dx in enumerate((2, 1, 3)):
        waits.append(
            send(
                depth_row.at[x], depth_row.at[x], drow_send.at[i], drow_recv.at[x], at_plane(in_plane(dx, 0))
            )
        )

    for dz in LINE:
        of = (z + dz) % NZ
        received(first_line.at[of], fline_recv.at[of])
    first_whole[core] = jnp.sum(first_line[...], axis=0)
    back_first = send(
        first_whole.at[core], first_whole.at[core], pair_send.at[3], pair_recv.at[3], sibling
    )

    for dx in (2, 1, 3):
        of = (x + dx) % NX
        received(depth_row.at[of], drow_recv.at[of])
    back_depth = send(depth_row, depth_back, pair_send.at[4], pair_recv.at[4], sibling)

    def unpack(packed):
        return packed[:, 0:40], pltpu.roll(packed, 64, 1)[:, 0:40]

    for dx, dy in PLANE:
        of = in_plane(dx, dy)
        received(second_plane.at[of], splane_recv.at[of])
    low, high = unpack(jnp.sum(second_plane[...], axis=0))
    out_second[0:32, :] = low
    out_second[32:64, :] = high

    for dz in LINE:
        of = (z + dz) % NZ
        received(core_line.at[of], line_recv.at[of])
    own, other = second_pack[32:40, 0:2], second_var[32:40, 0:2]
    own, other = jnp.where(half == 0, own[0:2], own[2:4]), jnp.where(half == 0, other[0:2], other[2:4])
    scales = (jnp.where(half == 0, own, other), jnp.where(half == 0, other, own))
    result = [jnp.zeros((8, 48), F32), jnp.zeros((8, 48), F32)]
    last = [jnp.zeros((1, 48), F32), jnp.zeros((1, 48), F32)]
    for h in range(2):
        tile = jnp.sum(core_line[h * HALF : h * HALF + HALF], axis=0)
        lanes = iota((1, 128), 1)
        ninth = jnp.where(
            lanes < 32,
            pltpu.roll(tile, 32, 1)[0:1],
            jnp.where(lanes < 64, pltpu.roll(tile, 64, 1)[1:2], pltpu.roll(tile, 96, 1)[2:3]),
        )
        ninth = jnp.broadcast_to(ninth, (8, 128))
        for v in range(2):
            tile_v = (pltpu.roll(tile, 80, 1) if v else tile)[:, 0:48]
            ninth_v = (pltpu.roll(ninth, 80, 1) if v else ninth)[0:1, 0:48]
            for w in range(2):
                scale = scales[h][w : w + 1, v : v + 1]
                result[w] = result[w] + scale * tile_v
                last[w] = last[w] + scale * ninth_v
    for w in range(2):
        for at in range(9):
            out_core[w, at % 3, at // 3 : at // 3 + 1, :] = result[w][at : at + 1, :] if at < 8 else last[w]

    back_first.wait_recv()
    low, high = unpack(first_whole[...].reshape(32, 128))
    out_first[0:32, :] = low
    out_first[32:64, :] = high

    back_depth.wait_recv()
    mine, theirs = depth_row[...], depth_back[...]
    firsts = jnp.where(core == 0, mine, theirs)
    seconds = jnp.where(core == 0, theirs, mine)
    pad[...] = zeros
    for g in range(4):
        pad[5 * g : 5 * g + 5, :] = firsts[g, 0:5, :]
        pad[20 + 5 * g : 25 + 5 * g, :] = seconds[g, 0:5, :]
    out_depth[...] = pad[...].T[:, 0:40]

    for copy in waits + pair_core + [pair_depth, pair_first, pair_var, back_first, back_depth]:
        copy.wait_send()


def on_device(*args):
    vmem = pl.BlockSpec(memory_space=pltpu.VMEM)
    dma = pltpu.SemaphoreType.DMA
    return pl.pallas_call(
        kernel,
        name="tucker",
        out_shape=(
            jax.ShapeDtypeStruct((64, 40), F32),
            jax.ShapeDtypeStruct((64, 40), F32),
            jax.ShapeDtypeStruct((128, 40), F32),
            jax.ShapeDtypeStruct((2, 3, 3, 48), F32),
        ),
        in_specs=[pl.BlockSpec(memory_space=pl.ANY)] + [vmem] * 8,
        out_specs=(vmem,) * 4,
        scratch_shapes=[
            pltpu.VMEM((2, 64, 64, 128), BF16),
            pltpu.VMEM((128, 128), F32),
            pltpu.VMEM((256, 256), BF16),
            pltpu.VMEM((192, 256), BF16),
            pltpu.VMEM((128, 768), BF16),
            pltpu.VMEM((64 * 48, 128), F32),
            pltpu.VMEM((768, 256), BF16),
            pltpu.VMEM((64, 128), F32),
            pltpu.VMEM((64, 128), F32),
            pltpu.VMEM((40, 64), BF16),
            pltpu.VMEM((40, 128), F32),
            pltpu.VMEM((2, 40, 128), F32),
            pltpu.VMEM((64, 128), F32),
            pltpu.VMEM((64, 128), F32),
            pltpu.VMEM((CHUNKS, GX, ZC, 8, 128), F32),
            pltpu.VMEM((CHUNKS, GX, ZC, 8, 128), F32),
            pltpu.VMEM((CHUNKS, GX, ZC, 8, 128), F32),
            pltpu.VMEM((CHUNKS, GX, ZC, 8, 128), F32),
            pltpu.VMEM((CHUNKS, GX, ZC, 8, 128), F32),
            pltpu.VMEM((HALF, 8, 128), F32),
            pltpu.VMEM((NZ, 8, 128), F32),
            pltpu.VMEM((8, 8, 128), F32),
            pltpu.VMEM((4, 8, 128), F32),
            pltpu.VMEM((4, 8, 128), F32),
            pltpu.VMEM((GX, 8, 128), F32),
            pltpu.VMEM((8, 128), F32),
            pltpu.VMEM((NZ, 8, 128), F32),
            pltpu.VMEM((NX, 8, 128), F32),
            pltpu.VMEM((NX, 8, 128), F32),
            pltpu.VMEM((2, 16, 128), F32),
            pltpu.VMEM((16, 128), F32),
            pltpu.VMEM((16, 128), F32),
            pltpu.VMEM((NZ, 16, 128), F32),
            pltpu.VMEM((2, 16, 128), F32),
            pltpu.VMEM((40, 128), F32),
            pltpu.VMEM((40, 128), F32),
            pltpu.VMEM((32, 128), F32),
            pltpu.VMEM((GX, 32, 128), F32),
            dma((8,)),
            dma((5,)),
            dma((5,)),
            dma((CHUNKS,)),
            dma((CHUNKS,)),
            dma((CHUNKS, 15)),
            dma((CHUNKS, GX)),
            dma((15,)),
            dma((NZ,)),
            dma((15,)),
            dma((GX,)),
            dma((15,)),
            dma((NZ,)),
            dma((3,)),
            dma((NX,)),
            dma((15,)),
            dma((NZ,)),
            dma((15,)),
            dma((GX,)),
        ],
        compiler_params=pltpu.CompilerParams(
            collective_id=0, has_side_effects=True, vmem_limit_bytes=32 << 20
        ),
        cost_estimate=pl.CostEstimate(flops=2_000_000_000, bytes_accessed=3_000_000, transcendentals=0),
    )(*args)


def solution(mesh):
    return jax.shard_map(
        on_device,
        mesh=mesh,
        in_specs=(
            P("var", "gx", "gy", None),
            P("gx", None),
            P("gy", None),
            P(),
            P("var", None),
            P(None, "gx"),
            P(None, "gy"),
            P(),
            P(None, "var"),
        ),
        out_specs=(P("gx", None), P("gy", None), P(), P("var", "gx", "gy", None)),
        check_vma=False,
    )
```

```python
import jax
import jax.numpy as jnp
from jax import lax
from jax.experimental import pallas as pl
from jax.experimental.pallas import tpu as pltpu
from jax.sharding import PartitionSpec as P

F32 = jnp.float32
BF16 = jnp.bfloat16
MESH = pl.DeviceIdType.MESH

NX, NY, NZ = 4, 4, 16
GX = NX * NY
HALF = NZ // 2
PLANE = [
    (2, 2), (2, 1), (1, 2), (2, 3), (3, 2), (1, 1), (3, 3), (1, 3), (3, 1),
    (2, 0), (0, 2), (1, 0), (0, 1), (3, 0), (0, 3),
]
ROW = [(2, 0), (2, 1), (1, 0), (3, 0), (1, 1), (3, 1), (0, 1)]
LINE = [8, 7, 9, 6, 10, 5, 11, 4, 12, 3, 13, 2, 14, 1, 15]
CHUNKS = 2
ZC = HALF // CHUNKS
OFFSET = 2
LOADS = 4


def dot(a, b):
    return jnp.dot(a, b, preferred_element_type=F32)


def iota(shape, axis):
    return lax.broadcasted_iota(jnp.int32, shape, axis)


def kernel(
    field,
    probe_first_hbm,
    probe_second_hbm,
    probe_depth_hbm,
    probe_vars_hbm,
    shrink_first_hbm,
    shrink_second_hbm,
    shrink_depth_hbm,
    shrink_vars_hbm,
    out_first,
    out_second,
    out_depth,
    out_core,
    probe_first,
    probe_second,
    probe_depth,
    probe_vars,
    shrink_first,
    shrink_second,
    shrink_depth,
    shrink_vars,
    held,
    pad,
    joined,
    spread,
    mix,
    stage,
    mixed,
    tested,
    weight_first,
    weight_second,
    rows_first,
    rows_second,
    core_away,
    core_own,
    core_sib,
    core_sum,
    core_plane,
    core_tiles,
    core_line,
    depth_parts,
    depth_sib,
    depth_sum,
    depth_plane,
    depth_tile,
    depth_line,
    depth_all,
    first_pack,
    first_sib,
    first_sum,
    first_line,
    first_whole,
    second_pack,
    second_var,
    second_sum,
    second_plane,
    small_sem,
    load_sem,
    pair_send,
    pair_recv,
    core_send,
    core_recv,
    plane_send,
    plane_recv,
    many_send,
    many_recv,
):
    gx, gy, half = lax.axis_index("gx"), lax.axis_index("gy"), lax.axis_index("var")
    x, y = gx // NY, gx % NY
    z_low, core = gy // 2, gy % 2
    z = half * HALF + z_low

    def in_plane(dx, dy):
        return ((x + dx) % NX) * NY + (y + dy) % NY

    def at_plane(there):
        return (there, gy, half)

    def at_line(there):
        return (gx, (there % HALF) * 2 + core, there // HALF)

    sibling = (gx, gy + 1 - 2 * core, half)
    partner = (gx, gy, 1 - half)
    row_peers = [(in_plane(dx, 0), gy + turn * (1 - 2 * core), half) for dx, turn in ROW]

    small = [
        pltpu.make_async_copy(src, dst, small_sem.at[i])
        for i, (src, dst) in enumerate(
            (
                (probe_first_hbm, probe_first),
                (probe_second_hbm, probe_second),
                (probe_vars_hbm, probe_vars),
                (probe_depth_hbm, probe_depth),
                (shrink_depth_hbm, shrink_depth),
                (shrink_second_hbm, shrink_second),
                (shrink_first_hbm, shrink_first),
                (shrink_vars_hbm, shrink_vars),
            )
        )
    ]
    for copy in small:
        copy.start()

    def load(part):
        rows = pl.ds(part * (64 // LOADS), 64 // LOADS)
        return pltpu.make_async_copy(field.at[:, rows], held.at[:, rows], load_sem.at[part])

    for part in range(LOADS):
        load(part).start()

    barrier = pltpu.get_barrier_semaphore()
    for dz in LINE:
        pl.semaphore_signal(barrier, inc=1, device_id=at_line((z + dz) % NZ), device_id_type=MESH)
    for dx, dy in PLANE:
        pl.semaphore_signal(barrier, inc=1, device_id=at_plane(in_plane(dx, dy)), device_id_type=MESH)
    for device, (dx, turn) in zip(row_peers, ROW):
        if turn:
            pl.semaphore_signal(barrier, inc=1, device_id=device, device_id_type=MESH)

    def send(src, dst, send_sem, recv_sem, device):
        copy = pltpu.make_async_remote_copy(
            src_ref=src, dst_ref=dst, send_sem=send_sem, recv_sem=recv_sem, device_id=device, device_id_type=MESH
        )
        copy.start()
        return copy

    def all_of(ref, sem):
        return pltpu.make_async_remote_copy(
            src_ref=ref, dst_ref=ref, send_sem=sem, recv_sem=sem, device_id=sibling, device_id_type=MESH
        )

    lane = iota((128, 128), 1)
    row = iota((128, 128), 0)
    zeros = jnp.zeros((128, 128), F32)

    for copy in small:
        copy.wait()

    def twice_turned(rows, offset):
        count, length = rows.shape
        pad[...] = zeros
        pad[0:count, 0:length] = rows
        pad[offset : offset + count, 0:length] = rows
        return pad[...].T

    pad[...] = zeros
    pad[0:2, 0:40] = probe_vars[...].astype(F32)
    both = pad[0:8, :]
    vars_row = both[0:1, :] + pltpu.roll(both, 64, 1)[1:2, :]
    tall = jnp.where(row < 64, both[0:1, :], both[1:2, :]).T[0:40, :]
    turned = pltpu.roll(tall, 64, 1)
    tall_vars = (
        jnp.where(iota((40, 128), 1) < 64, tall, turned),
        jnp.where(iota((40, 128), 1) < 64, turned, tall),
    )
    pad[...] = zeros
    pad[0:40, 0:64] = probe_second[...].astype(F32)
    wide = pad[0:40, :]
    tall_second = wide + pltpu.roll(wide, 64, 1)
    for g in range(8):
        lanes = iota((64, 512), 1)
        pick = jnp.where(iota((64, 512), 0) == g * 8 + lanes // 64, 1.0, 0.0).astype(BF16)
        firsts = dot(probe_first[...], pick)
        for q in range(4):
            product = firsts[:, q * 128 : q * 128 + 128] * tall_second
            for v in range(2):
                tested[v, :, g * 512 + q * 128 : g * 512 + q * 128 + 128] = (product * tall_vars[v]).astype(BF16)

    weight_first[...] = twice_turned(probe_first[...].astype(F32), 64)[0:64, :] * vars_row
    weight_second[...] = twice_turned(probe_second[...].astype(F32), 64)[0:64, :] * vars_row
    wide = twice_turned(probe_depth[...].astype(F32), 64)
    joined[0:128, 128:256] = jnp.where(lane < 64, wide, 0.0).astype(BF16)
    joined[128:256, 128:256] = jnp.where(lane >= 64, wide, 0.0).astype(BF16)
    wide = twice_turned(shrink_depth[...].astype(F32), 48)
    joined[0:128, 0:128] = jnp.where(lane < 48, wide, 0.0).astype(BF16)
    joined[128:256, 0:128] = jnp.where(lane >= 48, wide, 0.0).astype(BF16)

    pad[...] = zeros
    pad[0:48, 0:64] = shrink_second[...].astype(F32)
    block = pad[0:48, :]
    turned = pltpu.roll(block, 64, 1).astype(BF16)
    block = block.astype(BF16)
    for q in range(4):
        here, there = (q // 2) * 128, (1 - q // 2) * 128
        spread[q * 48 : q * 48 + 48, here : here + 128] = turned if q % 2 else block
        spread[q * 48 : q * 48 + 48, there : there + 128] = jnp.zeros((48, 128), BF16)

    pad[...] = zeros
    pad[0:48, 0:64] = shrink_first[...].astype(F32)
    wide = pad[0:48, :]
    twice = (wide + pltpu.roll(wide, 64, 1)).astype(BF16)
    at = iota((128, 48), 0)
    col = iota((128, 48), 1)
    each = dot(jnp.where(col == 3 * (at // 8) + (at % 8) % 3, 1.0, 0.0).astype(BF16), twice)
    ninth = dot(jnp.where(col == 3 * (at // 8) + 2, 1.0, 0.0).astype(BF16), twice)
    place = row % 8
    left = lane < 64
    third = place // 3
    blocks = [
        jnp.where(third == jnp.where(left, 0, 1), each, 0.0),
        jnp.where(left, jnp.where(third == 2, each, 0.0), jnp.where(place == 0, ninth, 0.0)),
        jnp.where(place == jnp.where(left, 1, 2), ninth, 0.0),
    ]
    for q in range(3):
        mix[:, q * 128 : q * 128 + 128] = blocks[q].astype(BF16)
        mix[:, (q + 3) * 128 : (q + 3) * 128 + 128] = blocks[q].astype(BF16)

    second_pack[...] = jnp.zeros((32, 128), F32)
    first_pack[...] = jnp.zeros((2, 16, 128), F32)
    second_pack[24:26, 0:4] = shrink_vars[...].astype(F32)
    depth_parts[...] = jnp.zeros((8, 8, 128), F32)

    depth_total = jnp.zeros((40, 128), F32)
    step = 64 // LOADS
    for part in range(LOADS):
        load(part).wait()
        for v in range(2):
            depth_total = depth_total + dot(
                tested[v, :, part * step * 64 : (part + 1) * step * 64],
                held[v, part * step : (part + 1) * step].reshape(step * 64, 128),
            )
    for g in range(8):
        depth_parts[g, 0:5, :] = depth_total[5 * g : 5 * g + 5, :]

    pl.semaphore_wait(barrier, len(LINE) + len(PLANE) + 4)

    pair_depth = send(
        depth_parts.at[pl.ds((1 - core) * 4, 4)], depth_sib, pair_send.at[0], pair_recv.at[0], sibling
    )

    def field_step(g, total):
        flat = jnp.concatenate(
            [held[v, g * 8 : g * 8 + 8].reshape(512, 128) for v in range(2)], axis=1
        )
        product = dot(flat, joined[...])
        compressed = product[:, 0:128].astype(BF16)
        probed = product[:, 128:256].reshape(8, 64, 128)
        for q in range(2):
            stage[g * 384 + q * 192 : g * 384 + q * 192 + 192, :] = dot(
                spread[...], compressed[q * 256 : q * 256 + 256, :]
            )
        firsts = weight_first[g * 8 : g * 8 + 8, :]
        seconds = weight_second[...]
        sums = []
        for i in range(8):
            total = total + probed[i] * firsts[i : i + 1, :]
            sums.append(jnp.sum(probed[i] * seconds, axis=0, keepdims=True))
        rows_first[g * 8 : g * 8 + 8, :] = jnp.concatenate(sums, axis=0)
        return total

    second_total = jnp.zeros((64, 128), F32)
    for g in range(4):
        second_total = field_step(g, second_total)

    pair_depth.wait_recv()
    depth_sum[...] = depth_parts[pl.ds(core * 4, 4)] + depth_sib[...]
    for dx, dy in PLANE:
        to = in_plane(dx, dy)
        send(depth_sum.at[to // NY], depth_plane.at[gx], many_send.at[0], many_recv.at[0], at_plane(to))
    depth_plane[gx] = depth_sum[x]

    for g in range(4, 8):
        second_total = field_step(g, second_total)
    rows_second[...] = second_total

    def pack(rows):
        rows = rows + pltpu.roll(rows, 64, 1)
        pad[0:64, :] = rows
        pad[64:128, :] = pltpu.roll(rows, 108, 1)
        return pad[...].T[0:20, :]

    packed = pack(rows_first[...])
    first_pack[0, 0:10, :] = packed[0:10, :]
    first_pack[1, 0:10, :] = packed[10:20, :]
    second_pack[0:20, :] = pack(rows_second[...])

    pair_first = send(first_pack.at[1 - core], first_sib, pair_send.at[1], pair_recv.at[1], sibling)
    pair_var = send(second_pack, second_var, pair_send.at[2], pair_recv.at[2], partner)

    def core_step(side, target, q):
        for s in range(ZC // 2):
            for t in range(2):
                place = (z_low + HALF - OFFSET + q * ZC + s * 2 + t) % HALF
                for b in range(3):
                    part = stage[pl.ds(place * 6 + 3 * side + b, 64, stride=48), :]
                    parts = [(b, part)]
                    if b == 2:
                        for u in range(3):
                            moved = pltpu.roll(part, 96 - 32 * u, 1)
                            parts.append((3 + u, jnp.where(iota((64, 128), 1) >= 96, moved, 0.0)))
                    for at, value in parts:
                        high = value.astype(BF16)
                        low = (value - high.astype(F32)).astype(BF16)
                        mixed[s, at * 64 : at * 64 + 64, t * 128 : t * 128 + 128] = high
                        mixed[s, 384 + at * 64 : 384 + at * 64 + 64, t * 128 : t * 128 + 128] = low
            result = dot(mix[...], mixed[s])
            for t in range(2):
                target[q, :, s * 2 + t] = result[:, t * 128 : t * 128 + 128].reshape(GX, 8, 128)

    pair_core = []
    for q in range(CHUNKS):
        core_step(1 - core, core_away, q)
        pair_core.append(send(core_away.at[q], core_sib.at[q], core_send.at[q], core_recv.at[q], sibling))
    for q in range(CHUNKS):
        core_step(core, core_own, q)

    for q in range(CHUNKS):
        pair_core[q].wait_recv()
        core_sum[q] = core_own[q] + core_sib[q]
        for dx, dy in PLANE:
            to = in_plane(dx, dy)
            send(core_sum.at[q, to], core_plane.at[q, gx], plane_send.at[q], plane_recv.at[q], at_plane(to))
        core_plane[q, gx] = core_sum[q, gx]

    pair_first.wait_recv()
    first_sum[...] = first_pack[core] + first_sib[...]
    for dz in LINE:
        send(
            first_sum.at[pl.ds(0, 8)],
            first_line.at[z],
            many_send.at[1],
            many_recv.at[1],
            at_line((z + dz) % NZ),
        )
    first_line[z] = first_sum[0:8, :]

    all_of(depth_plane.at[pl.ds(0, 15)], many_recv.at[0]).wait_recv()
    depth_tile[0:5, :] = jnp.sum(depth_plane[...], axis=0)[0:5, :]
    depth_tile[5:8, :] = first_sum[8:11, :]
    for dz in LINE:
        send(depth_tile, depth_line.at[z], many_send.at[2], many_recv.at[2], at_line((z + dz) % NZ))
    depth_line[z] = depth_tile[...]

    for q in range(CHUNKS):
        all_of(core_plane.at[q, pl.ds(0, 15)], plane_recv.at[q]).wait_recv()
        core_tiles[q] = jnp.sum(core_plane[q], axis=0)
        for far in (0, 1):
            for s in range(ZC):
                ahead = q * ZC + s - OFFSET
                if ahead == 0 and far:
                    continue
                to = (z + ahead + HALF * (1 - far) + NZ) % NZ
                send(core_tiles.at[q, s], core_line.at[z], many_send.at[3], many_recv.at[3], at_line(to))
        if q == 0:
            core_line[z] = core_tiles[0, OFFSET]
            pair_var.wait_recv()
            second_sum[...] = second_pack[0:24, :] + second_var[0:24, :]
            for dx, dy in PLANE:
                send(
                    second_sum,
                    second_plane.at[gx],
                    many_send.at[4],
                    many_recv.at[4],
                    at_plane(in_plane(dx, dy)),
                )
            second_plane[gx] = second_sum[...]

    mine = core * NX + x
    all_of(depth_line.at[pl.ds(0, 15)], many_recv.at[2]).wait_recv()
    depth_line_sum = jnp.sum(depth_line[...], axis=0)
    depth_all[mine] = depth_line_sum
    for device in row_peers:
        send(depth_all.at[mine], depth_all.at[mine], many_send.at[5], many_recv.at[5], device)

    all_of(first_line.at[pl.ds(0, 15)], many_recv.at[1]).wait_recv()
    first_whole[core, 0:8, :] = jnp.sum(first_line[...], axis=0)
    first_whole[core, 8:16, :] = pltpu.roll(depth_line_sum, 3, 0)
    back_first = send(
        first_whole.at[core], first_whole.at[core], pair_send.at[3], pair_recv.at[3], sibling
    )

    all_of(second_plane.at[pl.ds(0, 15)], many_recv.at[4]).wait_recv()
    packed = jnp.sum(second_plane[...], axis=0)
    out_second[0:20, :] = packed[0:20, 0:64]
    out_second[20:40, :] = pltpu.roll(packed, 64, 1)[0:20, 0:64]

    all_of(core_line.at[pl.ds(0, 15)], many_recv.at[3]).wait_recv()
    own, other = second_pack[24:32, 0:4], second_var[24:32, 0:4]
    own = jnp.where(half == 0, own[0:2, 0:2], own[0:2, 2:4])
    other = jnp.where(half == 0, other[0:2, 0:2], other[0:2, 2:4])
    scales = (jnp.where(half == 0, own, other), jnp.where(half == 0, other, own))
    result = [jnp.zeros((8, 48), F32), jnp.zeros((8, 48), F32)]
    last = [jnp.zeros((1, 48), F32), jnp.zeros((1, 48), F32)]
    for h in range(2):
        tile = jnp.sum(core_line[h * HALF : h * HALF + HALF], axis=0)
        lanes = iota((1, 128), 1)
        ninth = jnp.where(
            lanes < 32,
            pltpu.roll(tile, 32, 1)[0:1],
            jnp.where(lanes < 64, pltpu.roll(tile, 64, 1)[1:2], pltpu.roll(tile, 96, 1)[2:3]),
        )
        ninth = jnp.broadcast_to(ninth, (8, 128))
        for v in range(2):
            tile_v = (pltpu.roll(tile, 80, 1) if v else tile)[:, 0:48]
            ninth_v = (pltpu.roll(ninth, 80, 1) if v else ninth)[0:1, 0:48]
            for w in range(2):
                scale = scales[h][v : v + 1, w : w + 1]
                result[w] = result[w] + scale * tile_v
                last[w] = last[w] + scale * ninth_v
    for w in range(2):
        for at in range(9):
            out_core[at % 3, at // 3, w : w + 1, :] = result[w][at : at + 1, :] if at < 8 else last[w]

    back_first.wait_recv()
    for c in range(2):
        half_rows = first_whole[c]
        out_first[c * 10 : c * 10 + 10, :] = half_rows[0:10, 0:64]
        out_first[20 + c * 10 : 30 + c * 10, :] = pltpu.roll(half_rows, 64, 1)[0:10, 0:64]

    all_of(depth_all.at[pl.ds(0, 7)], many_recv.at[5]).wait_recv()
    for g in range(8):
        out_depth[5 * g : 5 * g + 5, :] = depth_all[g, 0:5, :]

    for copy in pair_core + [pair_depth, pair_first, pair_var, back_first]:
        copy.wait_send()
    for q in range(CHUNKS):
        all_of(core_sum.at[q, pl.ds(0, 15)], plane_send.at[q]).wait_send()
    for i, ref in enumerate((depth_plane, first_line, depth_line, core_line, second_plane)):
        all_of(ref.at[pl.ds(0, 15)], many_send.at[i]).wait_send()
    all_of(depth_all.at[pl.ds(0, 7)], many_send.at[5]).wait_send()


def finish(*refs):
    for i in range(4):
        refs[4 + i][...] = refs[i][...]


def on_device(
    field,
    probe_first,
    probe_second,
    probe_depth,
    probe_vars,
    shrink_first,
    shrink_second,
    shrink_depth,
    shrink_vars,
):
    vmem = pl.BlockSpec(memory_space=pltpu.VMEM)
    dma = pltpu.SemaphoreType.DMA
    shapes = (
        jax.ShapeDtypeStruct((40, 64), F32),
        jax.ShapeDtypeStruct((40, 64), F32),
        jax.ShapeDtypeStruct((40, 128), F32),
        jax.ShapeDtypeStruct((3, 3, 2, 48), F32),
    )
    results = pl.pallas_call(
        kernel,
        name="tucker",
        out_shape=shapes,
        in_specs=[pl.BlockSpec(memory_space=pltpu.HBM)] * 9,
        out_specs=(vmem,) * 4,
        scratch_shapes=[
            pltpu.VMEM((40, 64), BF16),
            pltpu.VMEM((40, 64), BF16),
            pltpu.VMEM((40, 128), BF16),
            pltpu.VMEM((2, 40), BF16),
            pltpu.VMEM((48, 64), BF16),
            pltpu.VMEM((48, 64), BF16),
            pltpu.VMEM((48, 128), BF16),
            pltpu.VMEM((2, 4), BF16),
            pltpu.VMEM((2, 64, 64, 128), BF16),
            pltpu.VMEM((128, 128), F32),
            pltpu.VMEM((256, 256), BF16),
            pltpu.VMEM((192, 256), BF16),
            pltpu.VMEM((128, 768), BF16),
            pltpu.VMEM((64 * 48, 128), F32),
            pltpu.VMEM((ZC // 2, 768, 256), BF16),
            pltpu.VMEM((2, 40, 4096), BF16),
            pltpu.VMEM((64, 128), F32),
            pltpu.VMEM((64, 128), F32),
            pltpu.VMEM((64, 128), F32),
            pltpu.VMEM((64, 128), F32),
            pltpu.VMEM((CHUNKS, GX, ZC, 8, 128), F32),
            pltpu.VMEM((CHUNKS, GX, ZC, 8, 128), F32),
            pltpu.VMEM((CHUNKS, GX, ZC, 8, 128), F32),
            pltpu.VMEM((CHUNKS, GX, ZC, 8, 128), F32),
            pltpu.VMEM((CHUNKS, GX, ZC, 8, 128), F32),
            pltpu.VMEM((CHUNKS, ZC, 8, 128), F32),
            pltpu.VMEM((NZ, 8, 128), F32),
            pltpu.VMEM((8, 8, 128), F32),
            pltpu.VMEM((4, 8, 128), F32),
            pltpu.VMEM((4, 8, 128), F32),
            pltpu.VMEM((GX, 8, 128), F32),
            pltpu.VMEM((8, 128), F32),
            pltpu.VMEM((NZ, 8, 128), F32),
            pltpu.VMEM((8, 8, 128), F32),
            pltpu.VMEM((2, 16, 128), F32),
            pltpu.VMEM((16, 128), F32),
            pltpu.VMEM((16, 128), F32),
            pltpu.VMEM((NZ, 8, 128), F32),
            pltpu.VMEM((2, 16, 128), F32),
            pltpu.VMEM((32, 128), F32),
            pltpu.VMEM((32, 128), F32),
            pltpu.VMEM((24, 128), F32),
            pltpu.VMEM((GX, 24, 128), F32),
            dma((8,)),
            dma((LOADS,)),
            dma((4,)),
            dma((4,)),
            dma((CHUNKS,)),
            dma((CHUNKS,)),
            dma((CHUNKS,)),
            dma((CHUNKS,)),
            dma((6,)),
            dma((6,)),
        ],
        compiler_params=pltpu.CompilerParams(
            collective_id=0, has_side_effects=True, vmem_limit_bytes=60 << 20
        ),
        cost_estimate=pl.CostEstimate(flops=2_000_000_000, bytes_accessed=3_000_000, transcendentals=0),
    )(
        field,
        probe_first.T,
        probe_second.T,
        probe_depth.T,
        probe_vars,
        shrink_first,
        shrink_second,
        shrink_depth,
        shrink_vars.T,
    )
    first, second, depth, core = pl.pallas_call(
        finish,
        name="finish",
        out_shape=shapes,
        in_specs=[vmem] * 4,
        out_specs=(vmem,) * 4,
        compiler_params=pltpu.CompilerParams(vmem_limit_bytes=60 << 20),
    )(*results)
    return first.T, second.T, depth.T, core.transpose(2, 0, 1, 3)


def solution(mesh):
    return jax.shard_map(
        on_device,
        mesh=mesh,
        in_specs=(
            P("var", "gx", "gy", None),
            P("gx", None),
            P("gy", None),
            P(),
            P("var", None),
            P(None, "gx"),
            P(None, "gy"),
            P(),
            P(None, "var"),
        ),
        out_specs=(P("gx", None), P("gy", None), P(), P("var", "gx", "gy", None)),
        check_vma=False,
    )
```

```python
import jax
import jax.numpy as jnp
from jax import lax
from jax.experimental import pallas as pl
from jax.experimental.pallas import tpu as pltpu
from jax.sharding import PartitionSpec as P

F32 = jnp.float32
BF16 = jnp.bfloat16
MESH = pl.DeviceIdType.MESH

NX, NY, NZ = 4, 4, 16
GX = NX * NY
HALF = NZ // 2
PLANE = [
    (2, 2), (2, 1), (1, 2), (2, 3), (3, 2), (1, 1), (3, 3), (1, 3), (3, 1),
    (2, 0), (0, 2), (1, 0), (0, 1), (3, 0), (0, 3),
]
ROW = [(2, 0), (2, 1), (1, 0), (3, 0), (1, 1), (3, 1), (0, 1)]
LINE = [8, 7, 9, 6, 10, 5, 11, 4, 12, 3, 13, 2, 14, 1, 15]
CHUNKS = 2
ZC = HALF // CHUNKS
OFFSET = 2
LOADS = 4
BEFORE = 7


def dot(a, b):
    return jnp.dot(a, b, preferred_element_type=F32)


def iota(shape, axis):
    return lax.broadcasted_iota(jnp.int32, shape, axis)


def kernel(
    field,
    probe_first_hbm,
    probe_second_hbm,
    probe_depth_hbm,
    probe_vars_hbm,
    shrink_first_hbm,
    shrink_second_hbm,
    shrink_depth_hbm,
    shrink_vars_hbm,
    out_first,
    out_second,
    out_depth,
    out_core,
    probe_first,
    probe_second,
    probe_depth,
    probe_vars,
    shrink_first,
    shrink_second,
    shrink_depth,
    shrink_vars,
    held,
    pad,
    joined,
    spread,
    mix,
    stage,
    mixed,
    tested,
    weight_first,
    weight_second,
    rows_first,
    rows_second,
    core_away,
    core_own,
    core_sib,
    core_sum,
    core_plane,
    core_tiles,
    core_line,
    depth_parts,
    depth_sib,
    depth_sum,
    depth_plane,
    depth_tile,
    depth_line,
    depth_all,
    first_pack,
    first_sib,
    first_sum,
    first_line,
    first_whole,
    second_pack,
    second_var,
    second_sum,
    second_plane,
    small_sem,
    load_sem,
    pair_send,
    pair_recv,
    core_send,
    core_recv,
    plane_send,
    plane_recv,
    many_send,
    many_recv,
):
    gx, gy, half = lax.axis_index("gx"), lax.axis_index("gy"), lax.axis_index("var")
    x, y = gx // NY, gx % NY
    z_low, core = gy // 2, gy % 2
    z = half * HALF + z_low

    def in_plane(dx, dy):
        return ((x + dx) % NX) * NY + (y + dy) % NY

    def at_plane(there):
        return (there, gy, half)

    def at_line(there):
        return (gx, (there % HALF) * 2 + core, there // HALF)

    sibling = (gx, gy + 1 - 2 * core, half)
    partner = (gx, gy, 1 - half)
    row_peers = [(in_plane(dx, 0), gy + turn * (1 - 2 * core), half) for dx, turn in ROW]

    small = [
        pltpu.make_async_copy(src, dst, small_sem.at[i])
        for i, (src, dst) in enumerate(
            (
                (probe_first_hbm, probe_first),
                (probe_second_hbm, probe_second),
                (probe_vars_hbm, probe_vars),
                (probe_depth_hbm, probe_depth),
                (shrink_depth_hbm, shrink_depth),
                (shrink_second_hbm, shrink_second),
                (shrink_first_hbm, shrink_first),
                (shrink_vars_hbm, shrink_vars),
            )
        )
    ]
    for copy in small:
        copy.start()

    def load(part):
        rows = pl.ds(part * (64 // LOADS), 64 // LOADS)
        return pltpu.make_async_copy(field.at[:, rows], held.at[:, rows], load_sem.at[part])

    for part in range(LOADS):
        load(part).start()

    barrier = pltpu.get_barrier_semaphore()
    for dz in LINE:
        pl.semaphore_signal(barrier, inc=1, device_id=at_line((z + dz) % NZ), device_id_type=MESH)
    for dx, dy in PLANE:
        pl.semaphore_signal(barrier, inc=1, device_id=at_plane(in_plane(dx, dy)), device_id_type=MESH)
    for device, (dx, turn) in zip(row_peers, ROW):
        if turn:
            pl.semaphore_signal(barrier, inc=1, device_id=device, device_id_type=MESH)

    def send(src, dst, send_sem, recv_sem, device):
        copy = pltpu.make_async_remote_copy(
            src_ref=src, dst_ref=dst, send_sem=send_sem, recv_sem=recv_sem, device_id=device, device_id_type=MESH
        )
        copy.start()
        return copy

    def all_of(ref, sem):
        return pltpu.make_async_remote_copy(
            src_ref=ref, dst_ref=ref, send_sem=sem, recv_sem=sem, device_id=sibling, device_id_type=MESH
        )

    lane = iota((128, 128), 1)
    row = iota((128, 128), 0)
    zeros = jnp.zeros((128, 128), F32)

    for copy in small:
        copy.wait()

    def twice_turned(rows, offset):
        count, length = rows.shape
        pad[...] = zeros
        pad[0:count, 0:length] = rows
        pad[offset : offset + count, 0:length] = rows
        return pad[...].T

    pad[...] = zeros
    pad[0:2, 0:40] = probe_vars[...].astype(F32)
    both = pad[0:8, :]
    vars_row = both[0:1, :] + pltpu.roll(both, 64, 1)[1:2, :]
    tall = jnp.where(row < 64, both[0:1, :], both[1:2, :]).T[0:40, :]
    turned = pltpu.roll(tall, 64, 1)
    tall_vars = (
        jnp.where(iota((40, 128), 1) < 64, tall, turned),
        jnp.where(iota((40, 128), 1) < 64, turned, tall),
    )
    pad[...] = zeros
    pad[0:40, 0:64] = probe_second[...].astype(F32)
    wide = pad[0:40, :]
    tall_second = wide + pltpu.roll(wide, 64, 1)
    for g in range(8):
        lanes = iota((64, 512), 1)
        pick = jnp.where(iota((64, 512), 0) == g * 8 + lanes // 64, 1.0, 0.0).astype(BF16)
        firsts = dot(probe_first[...], pick)
        for q in range(4):
            product = firsts[:, q * 128 : q * 128 + 128] * tall_second
            for v in range(2):
                tested[v, :, g * 512 + q * 128 : g * 512 + q * 128 + 128] = (product * tall_vars[v]).astype(BF16)

    weight_first[...] = twice_turned(probe_first[...].astype(F32), 64)[0:64, :] * vars_row
    weight_second[...] = twice_turned(probe_second[...].astype(F32), 64)[0:64, :] * vars_row
    wide = twice_turned(probe_depth[...].astype(F32), 64)
    joined[0:128, 128:256] = jnp.where(lane < 64, wide, 0.0).astype(BF16)
    joined[128:256, 128:256] = jnp.where(lane >= 64, wide, 0.0).astype(BF16)
    wide = twice_turned(shrink_depth[...].astype(F32), 48)
    joined[0:128, 0:128] = jnp.where(lane < 48, wide, 0.0).astype(BF16)
    joined[128:256, 0:128] = jnp.where(lane >= 48, wide, 0.0).astype(BF16)

    pad[...] = zeros
    pad[0:48, 0:64] = shrink_second[...].astype(F32)
    block = pad[0:48, :]
    turned = pltpu.roll(block, 64, 1).astype(BF16)
    block = block.astype(BF16)
    for q in range(4):
        here, there = (q // 2) * 128, (1 - q // 2) * 128
        spread[q * 48 : q * 48 + 48, here : here + 128] = turned if q % 2 else block
        spread[q * 48 : q * 48 + 48, there : there + 128] = jnp.zeros((48, 128), BF16)

    pad[...] = zeros
    pad[0:48, 0:64] = shrink_first[...].astype(F32)
    wide = pad[0:48, :]
    twice = (wide + pltpu.roll(wide, 64, 1)).astype(BF16)
    at = iota((128, 48), 0)
    col = iota((128, 48), 1)
    each = dot(jnp.where(col == 3 * (at // 8) + (at % 8) % 3, 1.0, 0.0).astype(BF16), twice)
    folded = dot(jnp.where(col == 3 * (at // 8) + 1 + (at % 8) // 3, 1.0, 0.0).astype(BF16), twice)
    place = row % 8
    left = lane < 64
    third = place // 3
    whole = place < 7
    short = place < 6
    turn = place % 3
    blocks = [
        jnp.where(whole & (third == jnp.where(left, 0, 1)), each, 0.0),
        jnp.where(left, jnp.where(place == 6, each, 0.0), jnp.where(short & (turn == 0), folded, 0.0)),
        jnp.where(short & (turn == jnp.where(left, 1, 2)), folded, 0.0),
    ]
    for q in range(3):
        mix[:, q * 128 : q * 128 + 128] = blocks[q].astype(BF16)
        mix[:, (q + 3) * 128 : (q + 3) * 128 + 128] = blocks[q].astype(BF16)

    second_pack[...] = jnp.zeros((24, 128), F32)
    first_pack[...] = jnp.zeros((2, 16, 128), F32)
    second_pack[20:22, 0:4] = shrink_vars[...].astype(F32)
    depth_parts[...] = jnp.zeros((8, 8, 128), F32)

    depth_total = jnp.zeros((40, 128), F32)
    step = 64 // LOADS
    for part in range(LOADS):
        load(part).wait()
        for v in range(2):
            depth_total = depth_total + dot(
                tested[v, :, part * step * 64 : (part + 1) * step * 64],
                held[v, part * step : (part + 1) * step].reshape(step * 64, 128),
            )
    for g in range(8):
        depth_parts[g, 0:5, :] = depth_total[5 * g : 5 * g + 5, :]

    def field_step(g, total):
        flat = jnp.concatenate(
            [held[v, g * 8 : g * 8 + 8].reshape(512, 128) for v in range(2)], axis=1
        )
        product = dot(flat, joined[...])
        compressed = product[:, 0:128].astype(BF16)
        probed = product[:, 128:256].reshape(8, 64, 128)
        for q in range(2):
            stage[g * 384 + q * 192 : g * 384 + q * 192 + 192, :] = dot(
                spread[...], compressed[q * 256 : q * 256 + 256, :]
            )
        firsts = weight_first[g * 8 : g * 8 + 8, :]
        seconds = weight_second[...]
        sums = []
        for i in range(8):
            total = total + probed[i] * firsts[i : i + 1, :]
            sums.append(jnp.sum(probed[i] * seconds, axis=0, keepdims=True))
        rows_first[g * 8 : g * 8 + 8, :] = jnp.concatenate(sums, axis=0)
        return total

    second_total = jnp.zeros((64, 128), F32)
    for g in range(BEFORE):
        second_total = field_step(g, second_total)

    pl.semaphore_wait(barrier, len(LINE) + len(PLANE) + 4)

    pair_depth = send(
        depth_parts.at[pl.ds((1 - core) * 4, 4)], depth_sib, pair_send.at[0], pair_recv.at[0], sibling
    )

    for g in range(BEFORE, BEFORE + 1):
        second_total = field_step(g, second_total)

    pair_depth.wait_recv()
    depth_sum[...] = depth_parts[pl.ds(core * 4, 4)] + depth_sib[...]
    for dx, dy in PLANE:
        to = in_plane(dx, dy)
        send(depth_sum.at[to // NY], depth_plane.at[gx], many_send.at[0], many_recv.at[0], at_plane(to))
    depth_plane[gx] = depth_sum[x]

    for g in range(BEFORE + 1, 8):
        second_total = field_step(g, second_total)
    rows_second[...] = second_total

    def pack(rows):
        rows = rows + pltpu.roll(rows, 64, 1)
        pad[0:64, :] = rows
        pad[64:128, :] = pltpu.roll(rows, 108, 1)
        return pad[...].T[0:20, :]

    packed = pack(rows_first[...])
    first_pack[0, 0:10, :] = packed[0:10, :]
    first_pack[1, 0:10, :] = packed[10:20, :]
    second_pack[0:20, :] = pack(rows_second[...])

    pair_var = send(second_pack, second_var, pair_send.at[2], pair_recv.at[2], partner)
    pair_first = send(first_pack.at[1 - core], first_sib, pair_send.at[1], pair_recv.at[1], sibling)

    def core_step(side, target, q):
        for s in range(ZC // 2):
            for t in range(2):
                place = (z_low + HALF - OFFSET + q * ZC + s * 2 + t) % HALF
                for b in range(3):
                    part = stage[pl.ds(place * 6 + 3 * side + b, 64, stride=48), :]
                    parts = [(b, part)]
                    if b == 2:
                        for u in range(3):
                            moved = pltpu.roll(part, 96 - 32 * u, 1)
                            parts.append((3 + u, jnp.where(iota((64, 128), 1) >= 96, moved, 0.0)))
                    for at, value in parts:
                        high = value.astype(BF16)
                        low = (value - high.astype(F32)).astype(BF16)
                        mixed[s, at * 64 : at * 64 + 64, t * 128 : t * 128 + 128] = high
                        mixed[s, 384 + at * 64 : 384 + at * 64 + 64, t * 128 : t * 128 + 128] = low
            result = dot(mix[...], mixed[s])
            for t in range(2):
                target[q, :, s * 2 + t] = result[:, t * 128 : t * 128 + 128].reshape(GX, 8, 128)

    pair_core = []
    for q in range(CHUNKS):
        core_step(1 - core, core_away, q)
        pair_core.append(send(
                core_away.at[q, :, :, pl.ds(0, 7)],
                core_sib.at[q, :, :, pl.ds(0, 7)],
                core_send.at[q],
                core_recv.at[q],
                sibling,
            ))
    for q in range(CHUNKS):
        core_step(core, core_own, q)

    for q in range(CHUNKS):
        pair_core[q].wait_recv()
        core_sum[q] = core_own[q] + core_sib[q]
        for dx, dy in PLANE:
            to = in_plane(dx, dy)
            send(
                core_sum.at[q, to, :, pl.ds(0, 7)],
                core_plane.at[q, gx, :, pl.ds(0, 7)],
                plane_send.at[q],
                plane_recv.at[q],
                at_plane(to),
            )
        core_plane[q, gx] = core_sum[q, gx]

    pair_first.wait_recv()
    first_sum[...] = first_pack[core] + first_sib[...]
    for dz in LINE:
        send(
            first_sum.at[pl.ds(0, 8)],
            first_line.at[z],
            many_send.at[1],
            many_recv.at[1],
            at_line((z + dz) % NZ),
        )
    first_line[z] = first_sum[0:8, :]

    all_of(depth_plane.at[pl.ds(0, 15)], many_recv.at[0]).wait_recv()
    depth_tile[0:5, :] = jnp.sum(depth_plane[...], axis=0)[0:5, :]
    depth_tile[5:8, :] = first_sum[8:11, :]
    for dz in LINE:
        send(depth_tile, depth_line.at[z], many_send.at[2], many_recv.at[2], at_line((z + dz) % NZ))
    depth_line[z] = depth_tile[...]

    for q in range(CHUNKS):
        all_of(core_plane.at[q, pl.ds(0, 15), :, pl.ds(0, 7)], plane_recv.at[q]).wait_recv()
        core_tiles[q] = jnp.sum(core_plane[q], axis=0)
        for far in (0, 1):
            for s in range(ZC):
                ahead = q * ZC + s - OFFSET
                if ahead == 0 and far:
                    continue
                to = (z + ahead + HALF * (1 - far) + NZ) % NZ
                send(core_tiles.at[q, s], core_line.at[z], many_send.at[3], many_recv.at[3], at_line(to))
        if q == 0:
            core_line[z] = core_tiles[0, OFFSET]
            pair_var.wait_recv()
            second_sum[...] = second_pack[...] + second_var[...]
            for dx, dy in PLANE:
                send(
                    second_sum,
                    second_plane.at[gx],
                    many_send.at[4],
                    many_recv.at[4],
                    at_plane(in_plane(dx, dy)),
                )
            second_plane[gx] = second_sum[...]

    mine = core * NX + x
    all_of(depth_line.at[pl.ds(0, 15)], many_recv.at[2]).wait_recv()
    depth_line_sum = jnp.sum(depth_line[...], axis=0)
    depth_all[mine] = depth_line_sum
    for device in row_peers:
        send(depth_all.at[mine], depth_all.at[mine], many_send.at[5], many_recv.at[5], device)

    all_of(first_line.at[pl.ds(0, 15)], many_recv.at[1]).wait_recv()
    first_whole[core, 0:8, :] = jnp.sum(first_line[...], axis=0)
    first_whole[core, 8:16, :] = pltpu.roll(depth_line_sum, 3, 0)
    back_first = send(
        first_whole.at[core], first_whole.at[core], pair_send.at[3], pair_recv.at[3], sibling
    )

    all_of(second_plane.at[pl.ds(0, 15)], many_recv.at[4]).wait_recv()
    packed = jnp.sum(second_plane[...], axis=0)
    out_second[0:20, :] = packed[0:20, 0:64]
    out_second[20:40, :] = pltpu.roll(packed, 64, 1)[0:20, 0:64]

    all_of(core_line.at[pl.ds(0, 15)], many_recv.at[3]).wait_recv()
    own, other = second_pack[16:24, 0:4][4:6], second_var[16:24, 0:4][4:6]
    own = jnp.where(half == 0, own[0:2, 0:2], own[0:2, 2:4])
    other = jnp.where(half == 0, other[0:2, 0:2], other[0:2, 2:4])
    scales = (jnp.where(half == 0, own, other), jnp.where(half == 0, other, own))
    result = [jnp.zeros((8, 48), F32), jnp.zeros((8, 48), F32)]
    last = [jnp.zeros((8, 48), F32), jnp.zeros((8, 48), F32)]
    lanes = iota((8, 128), 1)
    for h in range(2):
        tile = jnp.sum(core_line[h * HALF : h * HALF + HALF], axis=0)
        folded = jnp.where(
            lanes < 32,
            pltpu.roll(tile, 32, 1),
            jnp.where(
                lanes < 64,
                pltpu.roll(pltpu.roll(tile, 64, 1), 7, 0),
                pltpu.roll(pltpu.roll(tile, 96, 1), 6, 0),
            ),
        )
        for v in range(2):
            tile_v = (pltpu.roll(tile, 80, 1) if v else tile)[:, 0:48]
            folded_v = (pltpu.roll(folded, 80, 1) if v else folded)[:, 0:48]
            for w in range(2):
                scale = scales[h][v : v + 1, w : w + 1]
                result[w] = result[w] + scale * tile_v
                last[w] = last[w] + scale * folded_v
    for w in range(2):
        for at in range(9):
            source, of = (result[w], at) if at < 7 else (last[w], 3 * (at - 7))
            out_core[at % 3, at // 3, w : w + 1, :] = source[of : of + 1, :]

    back_first.wait_recv()
    for c in range(2):
        half_rows = first_whole[c]
        out_first[c * 10 : c * 10 + 10, :] = half_rows[0:10, 0:64]
        out_first[20 + c * 10 : 30 + c * 10, :] = pltpu.roll(half_rows, 64, 1)[0:10, 0:64]

    all_of(depth_all.at[pl.ds(0, 7)], many_recv.at[5]).wait_recv()
    for g in range(8):
        out_depth[5 * g : 5 * g + 5, :] = depth_all[g, 0:5, :]

    for copy in pair_core + [pair_depth, pair_first, pair_var, back_first]:
        copy.wait_send()
    for q in range(CHUNKS):
        all_of(core_sum.at[q, pl.ds(0, 15), :, pl.ds(0, 7)], plane_send.at[q]).wait_send()
    for i, ref in enumerate((depth_plane, first_line, depth_line, core_line, second_plane)):
        all_of(ref.at[pl.ds(0, 15)], many_send.at[i]).wait_send()
    all_of(depth_all.at[pl.ds(0, 7)], many_send.at[5]).wait_send()


def finish(*refs):
    for i in range(4):
        refs[4 + i][...] = refs[i][...]


def on_device(
    field,
    probe_first,
    probe_second,
    probe_depth,
    probe_vars,
    shrink_first,
    shrink_second,
    shrink_depth,
    shrink_vars,
):
    vmem = pl.BlockSpec(memory_space=pltpu.VMEM)
    dma = pltpu.SemaphoreType.DMA
    shapes = (
        jax.ShapeDtypeStruct((40, 64), F32),
        jax.ShapeDtypeStruct((40, 64), F32),
        jax.ShapeDtypeStruct((40, 128), F32),
        jax.ShapeDtypeStruct((3, 3, 2, 48), F32),
    )
    results = pl.pallas_call(
        kernel,
        name="tucker",
        out_shape=shapes,
        in_specs=[pl.BlockSpec(memory_space=pltpu.HBM)] * 9,
        out_specs=(vmem,) * 4,
        scratch_shapes=[
            pltpu.VMEM((40, 64), BF16),
            pltpu.VMEM((40, 64), BF16),
            pltpu.VMEM((40, 128), BF16),
            pltpu.VMEM((2, 40), BF16),
            pltpu.VMEM((48, 64), BF16),
            pltpu.VMEM((48, 64), BF16),
            pltpu.VMEM((48, 128), BF16),
            pltpu.VMEM((2, 4), BF16),
            pltpu.VMEM((2, 64, 64, 128), BF16),
            pltpu.VMEM((128, 128), F32),
            pltpu.VMEM((256, 256), BF16),
            pltpu.VMEM((192, 256), BF16),
            pltpu.VMEM((128, 768), BF16),
            pltpu.VMEM((64 * 48, 128), F32),
            pltpu.VMEM((ZC // 2, 768, 256), BF16),
            pltpu.VMEM((2, 40, 4096), BF16),
            pltpu.VMEM((64, 128), F32),
            pltpu.VMEM((64, 128), F32),
            pltpu.VMEM((64, 128), F32),
            pltpu.VMEM((64, 128), F32),
            pltpu.VMEM((CHUNKS, GX, ZC, 8, 128), F32),
            pltpu.VMEM((CHUNKS, GX, ZC, 8, 128), F32),
            pltpu.VMEM((CHUNKS, GX, ZC, 8, 128), F32),
            pltpu.VMEM((CHUNKS, GX, ZC, 8, 128), F32),
            pltpu.VMEM((CHUNKS, GX, ZC, 8, 128), F32),
            pltpu.VMEM((CHUNKS, ZC, 8, 128), F32),
            pltpu.VMEM((NZ, 8, 128), F32),
            pltpu.VMEM((8, 8, 128), F32),
            pltpu.VMEM((4, 8, 128), F32),
            pltpu.VMEM((4, 8, 128), F32),
            pltpu.VMEM((GX, 8, 128), F32),
            pltpu.VMEM((8, 128), F32),
            pltpu.VMEM((NZ, 8, 128), F32),
            pltpu.VMEM((8, 8, 128), F32),
            pltpu.VMEM((2, 16, 128), F32),
            pltpu.VMEM((16, 128), F32),
            pltpu.VMEM((16, 128), F32),
            pltpu.VMEM((NZ, 8, 128), F32),
            pltpu.VMEM((2, 16, 128), F32),
            pltpu.VMEM((24, 128), F32),
            pltpu.VMEM((24, 128), F32),
            pltpu.VMEM((24, 128), F32),
            pltpu.VMEM((GX, 24, 128), F32),
            dma((8,)),
            dma((LOADS,)),
            dma((4,)),
            dma((4,)),
            dma((CHUNKS,)),
            dma((CHUNKS,)),
            dma((CHUNKS,)),
            dma((CHUNKS,)),
            dma((6,)),
            dma((6,)),
        ],
        compiler_params=pltpu.CompilerParams(
            collective_id=0, has_side_effects=True, vmem_limit_bytes=60 << 20
        ),
        cost_estimate=pl.CostEstimate(flops=2_000_000_000, bytes_accessed=3_000_000, transcendentals=0),
    )(
        field,
        probe_first.T,
        probe_second.T,
        probe_depth.T,
        probe_vars,
        shrink_first,
        shrink_second,
        shrink_depth,
        shrink_vars.T,
    )
    first, second, depth, core = pl.pallas_call(
        finish,
        name="finish",
        out_shape=shapes,
        in_specs=[vmem] * 4,
        out_specs=(vmem,) * 4,
        compiler_params=pltpu.CompilerParams(vmem_limit_bytes=60 << 20),
    )(*results)
    return first.T, second.T, depth.T, core.transpose(2, 0, 1, 3)


def solution(mesh):
    return jax.shard_map(
        on_device,
        mesh=mesh,
        in_specs=(
            P("var", "gx", "gy", None),
            P("gx", None),
            P("gy", None),
            P(),
            P("var", None),
            P(None, "gx"),
            P(None, "gy"),
            P(),
            P(None, "var"),
        ),
        out_specs=(P("gx", None), P("gy", None), P(), P("var", "gx", "gy", None)),
        check_vma=False,
    )
```

```python
import jax
import jax.numpy as jnp
from jax import lax
from jax.experimental import pallas as pl
from jax.experimental.pallas import tpu as pltpu
from jax.sharding import PartitionSpec as P

F32 = jnp.float32
BF16 = jnp.bfloat16
MESH = pl.DeviceIdType.MESH

NX, NY, NZ = 4, 4, 16
GX = NX * NY
HALF = NZ // 2
PLANE = [
    (2, 2), (2, 1), (1, 2), (2, 3), (3, 2), (1, 1), (3, 3), (1, 3), (3, 1),
    (2, 0), (0, 2), (1, 0), (0, 1), (3, 0), (0, 3),
]
ROW = [(2, 0), (2, 1), (1, 0), (3, 0), (1, 1), (3, 1), (0, 1)]
LINE = [8, 7, 9, 6, 10, 5, 11, 4, 12, 3, 13, 2, 14, 1, 15]
CHUNKS = 2
ZC = HALF // CHUNKS
LOADS = 4
BEFORE = 3


def dot(a, b):
    return jnp.dot(a, b, preferred_element_type=F32)


def iota(shape, axis):
    return lax.broadcasted_iota(jnp.int32, shape, axis)


def kernel(
    field,
    probe_first_hbm,
    probe_second_hbm,
    probe_depth_hbm,
    probe_vars_hbm,
    shrink_first_hbm,
    shrink_second_hbm,
    shrink_depth_hbm,
    shrink_vars_hbm,
    out_first,
    out_second,
    out_depth,
    out_core,
    probe_first,
    probe_second,
    probe_depth,
    probe_vars,
    shrink_first,
    shrink_second,
    shrink_depth,
    shrink_vars,
    held,
    pad,
    joined,
    spread,
    mix,
    stage,
    mixed,
    tested,
    weight_first,
    weight_second,
    rows_first,
    rows_second,
    core_away,
    core_own,
    core_sib,
    core_sum,
    core_plane,
    core_tiles,
    core_line,
    depth_parts,
    depth_plane,
    depth_tile,
    depth_line,
    depth_all,
    first_pack,
    first_sib,
    first_sum,
    first_line,
    first_whole,
    second_pack,
    second_var,
    second_sum,
    second_plane,
    small_sem,
    load_sem,
    pair_send,
    pair_recv,
    core_send,
    core_recv,
    plane_send,
    plane_recv,
    many_send,
    many_recv,
):
    gx, gy, half = lax.axis_index("gx"), lax.axis_index("gy"), lax.axis_index("var")
    x, y = gx // NY, gx % NY
    z_low, core = gy // 2, gy % 2
    z = half * HALF + z_low

    def in_plane(dx, dy):
        return ((x + dx) % NX) * NY + (y + dy) % NY

    def at_plane(there):
        return (there, gy, half)

    def at_line(there):
        return (gx, (there % HALF) * 2 + core, there // HALF)

    mine = core * NX + x
    sibling = (gx, gy + 1 - 2 * core, half)
    partner = (gx, gy, 1 - half)
    row_peers = [(in_plane(dx, 0), gy + turn * (1 - 2 * core), half) for dx, turn in ROW]

    small = [
        pltpu.make_async_copy(src, dst, small_sem.at[i])
        for i, (src, dst) in enumerate(
            (
                (probe_first_hbm, probe_first),
                (probe_second_hbm, probe_second),
                (probe_vars_hbm, probe_vars),
                (probe_depth_hbm, probe_depth),
                (shrink_depth_hbm, shrink_depth),
                (shrink_second_hbm, shrink_second),
                (shrink_first_hbm, shrink_first),
                (shrink_vars_hbm, shrink_vars),
            )
        )
    ]
    for copy in small:
        copy.start()

    def load(part):
        rows = pl.ds(part * (64 // LOADS), 64 // LOADS)
        return pltpu.make_async_copy(field.at[:, rows], held.at[:, rows], load_sem.at[part])

    for part in range(LOADS):
        load(part).start()

    barrier = pltpu.get_barrier_semaphore()
    for dz in LINE:
        pl.semaphore_signal(barrier, inc=1, device_id=at_line((z + dz) % NZ), device_id_type=MESH)
    for dx, dy in PLANE:
        pl.semaphore_signal(barrier, inc=1, device_id=at_plane(in_plane(dx, dy)), device_id_type=MESH)
        other = (in_plane(dx, dy), gy + 1 - 2 * core, half)
        pl.semaphore_signal(barrier, inc=1, device_id=other, device_id_type=MESH)
    pl.semaphore_signal(barrier, inc=1, device_id=sibling, device_id_type=MESH)

    def send(src, dst, send_sem, recv_sem, device):
        copy = pltpu.make_async_remote_copy(
            src_ref=src, dst_ref=dst, send_sem=send_sem, recv_sem=recv_sem, device_id=device, device_id_type=MESH
        )
        copy.start()
        return copy

    def all_of(ref, sem):
        return pltpu.make_async_remote_copy(
            src_ref=ref, dst_ref=ref, send_sem=sem, recv_sem=sem, device_id=sibling, device_id_type=MESH
        )

    lane = iota((128, 128), 1)
    row = iota((128, 128), 0)
    zeros = jnp.zeros((128, 128), F32)

    for copy in small:
        copy.wait()

    def twice_turned(rows, offset):
        count, length = rows.shape
        pad[...] = zeros
        pad[0:count, 0:length] = rows
        pad[offset : offset + count, 0:length] = rows
        return pad[...].T

    pad[...] = zeros
    pad[0:2, 0:40] = probe_vars[...].astype(F32)
    both = pad[0:8, :]
    vars_row = both[0:1, :] + pltpu.roll(both, 64, 1)[1:2, :]
    tall = jnp.where(row < 64, both[0:1, :], both[1:2, :]).T[0:40, :]
    turned = pltpu.roll(tall, 64, 1)
    tall_vars = (
        jnp.where(iota((40, 128), 1) < 64, tall, turned),
        jnp.where(iota((40, 128), 1) < 64, turned, tall),
    )
    pad[...] = zeros
    pad[0:40, 0:64] = probe_second[...].astype(F32)
    wide = pad[0:40, :]
    tall_second = wide + pltpu.roll(wide, 64, 1)
    for g in range(8):
        lanes = iota((64, 512), 1)
        pick = jnp.where(iota((64, 512), 0) == g * 8 + lanes // 64, 1.0, 0.0).astype(BF16)
        firsts = dot(probe_first[...], pick)
        for q in range(4):
            product = firsts[:, q * 128 : q * 128 + 128] * tall_second
            for v in range(2):
                tested[v, :, g * 512 + q * 128 : g * 512 + q * 128 + 128] = (product * tall_vars[v]).astype(BF16)

    weight_first[...] = twice_turned(probe_first[...].astype(F32), 64)[0:64, :] * vars_row
    weight_second[...] = twice_turned(probe_second[...].astype(F32), 64)[0:64, :] * vars_row
    wide = twice_turned(probe_depth[...].astype(F32), 64)
    joined[0:128, 128:256] = jnp.where(lane < 64, wide, 0.0).astype(BF16)
    joined[128:256, 128:256] = jnp.where(lane >= 64, wide, 0.0).astype(BF16)
    wide = twice_turned(shrink_depth[...].astype(F32), 48)
    joined[0:128, 0:128] = jnp.where(lane < 48, wide, 0.0).astype(BF16)
    joined[128:256, 0:128] = jnp.where(lane >= 48, wide, 0.0).astype(BF16)

    pad[...] = zeros
    pad[0:48, 0:64] = shrink_second[...].astype(F32)
    block = pad[0:48, :]
    turned = pltpu.roll(block, 64, 1).astype(BF16)
    block = block.astype(BF16)
    for q in range(4):
        here, there = (q // 2) * 128, (1 - q // 2) * 128
        spread[q * 48 : q * 48 + 48, here : here + 128] = turned if q % 2 else block
        spread[q * 48 : q * 48 + 48, there : there + 128] = jnp.zeros((48, 128), BF16)

    pad[...] = zeros
    pad[0:48, 0:64] = shrink_first[...].astype(F32)
    wide = pad[0:48, :]
    twice = (wide + pltpu.roll(wide, 64, 1)).astype(BF16)
    at = iota((128, 48), 0)
    col = iota((128, 48), 1)
    each = dot(jnp.where(col == 3 * (at // 8) + (at % 8) % 3, 1.0, 0.0).astype(BF16), twice)
    folded = dot(jnp.where(col == 3 * (at // 8) + 1 + (at % 8) // 3, 1.0, 0.0).astype(BF16), twice)
    place = row % 8
    left = lane < 64
    third = place // 3
    whole = place < 7
    short = place < 6
    turn = place % 3
    blocks = [
        jnp.where(whole & (third == jnp.where(left, 0, 1)), each, 0.0),
        jnp.where(left, jnp.where(place == 6, each, 0.0), jnp.where(short & (turn == 0), folded, 0.0)),
        jnp.where(short & (turn == jnp.where(left, 1, 2)), folded, 0.0),
    ]
    for q in range(3):
        mix[:, q * 128 : q * 128 + 128] = blocks[q].astype(BF16)
        mix[:, (q + 3) * 128 : (q + 3) * 128 + 128] = blocks[q].astype(BF16)

    second_pack[...] = jnp.zeros((24, 128), F32)
    first_pack[...] = jnp.zeros((2, 16, 128), F32)
    second_pack[20:22, 0:4] = shrink_vars[...].astype(F32)
    depth_parts[...] = jnp.zeros((8, 8, 128), F32)

    depth_total = jnp.zeros((40, 128), F32)
    step = 64 // LOADS
    for part in range(LOADS):
        load(part).wait()
        for v in range(2):
            depth_total = depth_total + dot(
                tested[v, :, part * step * 64 : (part + 1) * step * 64],
                held[v, part * step : (part + 1) * step].reshape(step * 64, 128),
            )
    for g in range(8):
        depth_parts[g, 0:5, :] = depth_total[5 * g : 5 * g + 5, :]

    early = half == 0

    def meet():
        pl.semaphore_wait(barrier, len(LINE) + 2 * len(PLANE) + 1)

        for dx, dy in PLANE:
            to = in_plane(dx, dy)
            for turn in (0, 1):
                there = core + turn * (1 - 2 * core)
                send(
                    depth_parts.at[there * NX + to // NY],
                    depth_plane.at[core * GX + gx],
                    many_send.at[0],
                    many_recv.at[0],
                    (to, gy + turn * (1 - 2 * core), half),
                )
        send(
            depth_parts.at[(1 - core) * NX + x],
            depth_plane.at[core * GX + gx],
            many_send.at[0],
            many_recv.at[0],
            sibling,
        )
        depth_plane[core * GX + gx] = depth_parts[mine]

    def share():
        send(second_pack, second_var, pair_send.at[1], pair_recv.at[1], partner)
        send(first_pack.at[1 - core], first_sib, pair_send.at[0], pair_recv.at[0], sibling)

    def away(q):
        send(
            core_away.at[q, :, :, pl.ds(0, 7)],
            core_sib.at[q, :, :, pl.ds(0, 7)],
            core_send.at[q],
            core_recv.at[q],
            sibling,
        )

    def rows_of(g):
        return jnp.concatenate([held[v, g * 16 : g * 16 + 16].reshape(1024, 128) for v in range(2)], axis=1)

    def field_step(g, total):
        product = dot(rows_of(g), joined[...])
        compressed = product[:, 0:128].astype(BF16)
        probed = product[:, 128:256].reshape(16, 64, 128)
        for q in range(4):
            stage[g * 768 + q * 192 : g * 768 + q * 192 + 192, :] = dot(
                spread[...], compressed[q * 256 : q * 256 + 256, :]
            )
        firsts = weight_first[g * 16 : g * 16 + 16, :]
        seconds = weight_second[...]
        sums = []
        for i in range(16):
            total = total + probed[i] * firsts[i : i + 1, :]
            sums.append(jnp.sum(probed[i] * seconds, axis=0, keepdims=True))
        rows_first[g * 16 : g * 16 + 16, :] = jnp.concatenate(sums, axis=0)
        return total

    second_total = jnp.zeros((64, 128), F32)
    for g in range(BEFORE):
        second_total = field_step(g, second_total)
    pl.when(jnp.logical_not(early))(meet)
    for g in range(BEFORE, 4):
        second_total = field_step(g, second_total)
    rows_second[...] = second_total

    def pack(rows):
        rows = rows + pltpu.roll(rows, 64, 1)
        pad[0:64, :] = rows
        pad[64:128, :] = pltpu.roll(rows, 108, 1)
        return pad[...].T[0:20, :]

    packed = pack(rows_first[...])
    first_pack[0, 0:10, :] = packed[0:10, :]
    first_pack[1, 0:10, :] = packed[10:20, :]
    second_pack[0:20, :] = pack(rows_second[...])
    pl.when(jnp.logical_not(early))(share)

    def core_step(side, target, q):
        for s in range(ZC // 2):
            for t in range(2):
                place = (z_low + HALF - (q * ZC + s * 2 + t)) % HALF
                for b in range(3):
                    part = stage[pl.ds(place * 6 + 3 * side + b, 64, stride=48), :]
                    parts = [(b, part)]
                    if b == 2:
                        for u in range(3):
                            moved = pltpu.roll(part, 96 - 32 * u, 1)
                            parts.append((3 + u, jnp.where(iota((64, 128), 1) >= 96, moved, 0.0)))
                    for at, value in parts:
                        high = value.astype(BF16)
                        low = (value - high.astype(F32)).astype(BF16)
                        mixed[s, at * 64 : at * 64 + 64, t * 128 : t * 128 + 128] = high
                        mixed[s, 384 + at * 64 : 384 + at * 64 + 64, t * 128 : t * 128 + 128] = low
            result = dot(mix[...], mixed[s])
            for t in range(2):
                target[q, :, s * 2 + t] = result[:, t * 128 : t * 128 + 128].reshape(GX, 8, 128)

    for q in range(CHUNKS):
        core_step(1 - core, core_away, q)
        pl.when(jnp.logical_not(early))(lambda q=q: away(q))
    @pl.when(early)
    def _():
        meet()
        share()
        for q in range(CHUNKS):
            away(q)

    for q in range(CHUNKS):
        core_step(core, core_own, q)

    all_of(first_sib, pair_recv.at[0]).wait_recv()
    first_sum[...] = first_pack[core] + first_sib[...]
    for dz in LINE:
        send(
            first_sum.at[pl.ds(0, 8)],
            first_line.at[z],
            many_send.at[1],
            many_recv.at[1],
            at_line((z + dz) % NZ),
        )
    first_line[z] = first_sum[0:8, :]

    for q in range(CHUNKS):
        all_of(core_sib.at[q, :, :, pl.ds(0, 7)], core_recv.at[q]).wait_recv()
        core_sum[q] = core_own[q] + core_sib[q]
        for dx, dy in PLANE:
            to = in_plane(dx, dy)
            send(
                core_sum.at[q, to, :, pl.ds(0, 7)],
                core_plane.at[q, gx, :, pl.ds(0, 7)],
                plane_send.at[q],
                plane_recv.at[q],
                at_plane(to),
            )
        core_plane[q, gx] = core_sum[q, gx]

    all_of(depth_plane.at[pl.ds(0, 31)], many_recv.at[0]).wait_recv()
    depth_tile[0:5, :] = jnp.sum(depth_plane[...], axis=0)[0:5, :]
    depth_tile[5:8, :] = first_sum[8:11, :]
    for dz in LINE:
        send(depth_tile, depth_line.at[z], many_send.at[2], many_recv.at[2], at_line((z + dz) % NZ))
    depth_line[z] = depth_tile[...]

    for q in range(CHUNKS):
        all_of(core_plane.at[q, pl.ds(0, 15), :, pl.ds(0, 7)], plane_recv.at[q]).wait_recv()
        core_tiles[q] = jnp.sum(core_plane[q], axis=0)
        for far in (0, 1):
            for s in range(ZC):
                behind = q * ZC + s
                if behind == 0 and far:
                    continue
                to = (z + HALF * (1 + far) - behind) % NZ
                send(core_tiles.at[q, s], core_line.at[z], many_send.at[3], many_recv.at[3], at_line(to))
        if q == 0:
            core_line[z] = core_tiles[0, 0]
            all_of(second_var, pair_recv.at[1]).wait_recv()
            second_sum[...] = second_pack[...] + second_var[...]
            for dx, dy in PLANE:
                send(
                    second_sum,
                    second_plane.at[gx],
                    many_send.at[4],
                    many_recv.at[4],
                    at_plane(in_plane(dx, dy)),
                )
            second_plane[gx] = second_sum[...]

    all_of(depth_line.at[pl.ds(0, 15)], many_recv.at[2]).wait_recv()
    depth_line_sum = jnp.sum(depth_line[...], axis=0)
    depth_all[mine] = depth_line_sum
    for device in row_peers:
        send(depth_all.at[mine], depth_all.at[mine], many_send.at[5], many_recv.at[5], device)

    all_of(first_line.at[pl.ds(0, 15)], many_recv.at[1]).wait_recv()
    first_whole[core, 0:8, :] = jnp.sum(first_line[...], axis=0)
    first_whole[core, 8:16, :] = pltpu.roll(depth_line_sum, 3, 0)
    back_first = send(
        first_whole.at[core], first_whole.at[core], pair_send.at[2], pair_recv.at[2], sibling
    )

    all_of(second_plane.at[pl.ds(0, 15)], many_recv.at[4]).wait_recv()
    packed = jnp.sum(second_plane[...], axis=0)
    out_second[0:20, :] = packed[0:20, 0:64]
    out_second[20:40, :] = pltpu.roll(packed, 64, 1)[0:20, 0:64]

    all_of(core_line.at[pl.ds(0, 15)], many_recv.at[3]).wait_recv()
    own, other = second_pack[16:24, 0:4][4:6], second_var[16:24, 0:4][4:6]
    own = jnp.where(half == 0, own[0:2, 0:2], own[0:2, 2:4])
    other = jnp.where(half == 0, other[0:2, 0:2], other[0:2, 2:4])
    scales = (jnp.where(half == 0, own, other), jnp.where(half == 0, other, own))
    result = [jnp.zeros((8, 48), F32), jnp.zeros((8, 48), F32)]
    last = [jnp.zeros((8, 48), F32), jnp.zeros((8, 48), F32)]
    lanes = iota((8, 128), 1)
    for h in range(2):
        tile = jnp.sum(core_line[h * HALF : h * HALF + HALF], axis=0)
        folded = jnp.where(
            lanes < 32,
            pltpu.roll(tile, 32, 1),
            jnp.where(
                lanes < 64,
                pltpu.roll(pltpu.roll(tile, 64, 1), 7, 0),
                pltpu.roll(pltpu.roll(tile, 96, 1), 6, 0),
            ),
        )
        for v in range(2):
            tile_v = (pltpu.roll(tile, 80, 1) if v else tile)[:, 0:48]
            folded_v = (pltpu.roll(folded, 80, 1) if v else folded)[:, 0:48]
            for w in range(2):
                scale = scales[h][v : v + 1, w : w + 1]
                result[w] = result[w] + scale * tile_v
                last[w] = last[w] + scale * folded_v
    for w in range(2):
        for at in range(9):
            source, of = (result[w], at) if at < 7 else (last[w], 3 * (at - 7))
            out_core[at % 3, at // 3, w : w + 1, :] = source[of : of + 1, :]

    back_first.wait_recv()
    for c in range(2):
        half_rows = first_whole[c]
        out_first[c * 10 : c * 10 + 10, :] = half_rows[0:10, 0:64]
        out_first[20 + c * 10 : 30 + c * 10, :] = pltpu.roll(half_rows, 64, 1)[0:10, 0:64]

    all_of(depth_all.at[pl.ds(0, 7)], many_recv.at[5]).wait_recv()
    for g in range(8):
        out_depth[5 * g : 5 * g + 5, :] = depth_all[g, 0:5, :]

    back_first.wait_send()
    all_of(first_sib, pair_send.at[0]).wait_send()
    all_of(second_var, pair_send.at[1]).wait_send()
    for q in range(CHUNKS):
        all_of(core_sib.at[q, :, :, pl.ds(0, 7)], core_send.at[q]).wait_send()
    for q in range(CHUNKS):
        all_of(core_sum.at[q, pl.ds(0, 15), :, pl.ds(0, 7)], plane_send.at[q]).wait_send()
    all_of(depth_plane.at[pl.ds(0, 31)], many_send.at[0]).wait_send()
    for i, ref in enumerate((first_line, depth_line, core_line, second_plane)):
        all_of(ref.at[pl.ds(0, 15)], many_send.at[i + 1]).wait_send()
    all_of(depth_all.at[pl.ds(0, 7)], many_send.at[5]).wait_send()


def finish(*refs):
    for i in range(4):
        refs[4 + i][...] = refs[i][...]


def on_device(
    field,
    probe_first,
    probe_second,
    probe_depth,
    probe_vars,
    shrink_first,
    shrink_second,
    shrink_depth,
    shrink_vars,
):
    vmem = pl.BlockSpec(memory_space=pltpu.VMEM)
    dma = pltpu.SemaphoreType.DMA
    shapes = (
        jax.ShapeDtypeStruct((40, 64), F32),
        jax.ShapeDtypeStruct((40, 64), F32),
        jax.ShapeDtypeStruct((40, 128), F32),
        jax.ShapeDtypeStruct((3, 3, 2, 48), F32),
    )
    results = pl.pallas_call(
        kernel,
        name="tucker",
        out_shape=shapes,
        in_specs=[pl.BlockSpec(memory_space=pltpu.HBM)] * 9,
        out_specs=(vmem,) * 4,
        scratch_shapes=[
            pltpu.VMEM((40, 64), BF16),
            pltpu.VMEM((40, 64), BF16),
            pltpu.VMEM((40, 128), BF16),
            pltpu.VMEM((2, 40), BF16),
            pltpu.VMEM((48, 64), BF16),
            pltpu.VMEM((48, 64), BF16),
            pltpu.VMEM((48, 128), BF16),
            pltpu.VMEM((2, 4), BF16),
            pltpu.VMEM((2, 64, 64, 128), BF16),
            pltpu.VMEM((128, 128), F32),
            pltpu.VMEM((256, 256), BF16),
            pltpu.VMEM((192, 256), BF16),
            pltpu.VMEM((128, 768), BF16),
            pltpu.VMEM((64 * 48, 128), F32),
            pltpu.VMEM((ZC // 2, 768, 256), BF16),
            pltpu.VMEM((2, 40, 4096), BF16),
            pltpu.VMEM((64, 128), F32),
            pltpu.VMEM((64, 128), F32),
            pltpu.VMEM((64, 128), F32),
            pltpu.VMEM((64, 128), F32),
            pltpu.VMEM((CHUNKS, GX, ZC, 8, 128), F32),
            pltpu.VMEM((CHUNKS, GX, ZC, 8, 128), F32),
            pltpu.VMEM((CHUNKS, GX, ZC, 8, 128), F32),
            pltpu.VMEM((CHUNKS, GX, ZC, 8, 128), F32),
            pltpu.VMEM((CHUNKS, GX, ZC, 8, 128), F32),
            pltpu.VMEM((CHUNKS, ZC, 8, 128), F32),
            pltpu.VMEM((NZ, 8, 128), F32),
            pltpu.VMEM((8, 8, 128), F32),
            pltpu.VMEM((2 * GX, 8, 128), F32),
            pltpu.VMEM((8, 128), F32),
            pltpu.VMEM((NZ, 8, 128), F32),
            pltpu.VMEM((8, 8, 128), F32),
            pltpu.VMEM((2, 16, 128), F32),
            pltpu.VMEM((16, 128), F32),
            pltpu.VMEM((16, 128), F32),
            pltpu.VMEM((NZ, 8, 128), F32),
            pltpu.VMEM((2, 16, 128), F32),
            pltpu.VMEM((24, 128), F32),
            pltpu.VMEM((24, 128), F32),
            pltpu.VMEM((24, 128), F32),
            pltpu.VMEM((GX, 24, 128), F32),
            dma((8,)),
            dma((LOADS,)),
            dma((3,)),
            dma((3,)),
            dma((CHUNKS,)),
            dma((CHUNKS,)),
            dma((CHUNKS,)),
            dma((CHUNKS,)),
            dma((6,)),
            dma((6,)),
        ],
        compiler_params=pltpu.CompilerParams(
            collective_id=0, has_side_effects=True, vmem_limit_bytes=60 << 20
        ),
        cost_estimate=pl.CostEstimate(flops=2_000_000_000, bytes_accessed=3_000_000, transcendentals=0),
    )(
        field,
        probe_first.T,
        probe_second.T,
        probe_depth.T,
        probe_vars,
        shrink_first,
        shrink_second,
        shrink_depth,
        shrink_vars.T,
    )
    first, second, depth, core = pl.pallas_call(
        finish,
        name="finish",
        out_shape=shapes,
        in_specs=[vmem] * 4,
        out_specs=(vmem,) * 4,
        compiler_params=pltpu.CompilerParams(vmem_limit_bytes=60 << 20),
    )(*results)
    return first.T, second.T, depth.T, core.transpose(2, 0, 1, 3)


def solution(mesh):
    return jax.shard_map(
        on_device,
        mesh=mesh,
        in_specs=(
            P("var", "gx", "gy", None),
            P("gx", None),
            P("gy", None),
            P(),
            P("var", None),
            P(None, "gx"),
            P(None, "gy"),
            P(),
            P(None, "var"),
        ),
        out_specs=(P("gx", None), P("gy", None), P(), P("var", "gx", "gy", None)),
        check_vma=False,
    )
```
